32 devices in a mesh: sy: 4 (over x, core), sx: 4 (over z), ch: 2 (over y).
Axes of the slice: x: 2, y: 2, z: 4, core: 2. Of those that a mesh axis runs over, the one named last changes fastest.
Arguments:
- frames: bfloat16 [144, 144, 128], P('sy', 'sx'), may hold values from -6 to 6
- w_input: bfloat16 [9, 64, 4, 1024], P(None, None, None, 'ch'), may hold values from -0.25 to 0.25
- w_hidden: bfloat16 [9, 1024, 4, 1024], P(None, None, None, 'ch'), may hold values from -0.0625 to 0.0625
- biases: float32 [4, 1024], P(None, 'ch'), may hold values from -4 to 4
- hidden_init: bfloat16 [144, 144, 1024], P('sy', 'sx', 'ch'), may hold values from -1 to 1
- cell_init: float32 [144, 144, 1024], P('sy', 'sx', 'ch'), may hold values from -5 to 5
Outputs:
- hidden_out: bfloat16 [144, 144, 1024], P('sy', 'sx', 'ch')
- cell_out: float32 [144, 144, 1024], P('sy', 'sx', 'ch')
The draws below stay inside these ranges and needn't reach their ends.
All inputs are finite; a program needn't handle non-finite values.
Results may differ from the reference program's by a relative error of at most 0.0021.
Values may be sent and summed in bfloat16 or wider, within the bound.
No kernel may reach another device: no remote copies, remote signals or barrier semaphores. Data moves between devices by JAX's collectives and lax.ppermute only.
A program may use at most 448 MiB of HBM per device.

```python
import jax
import jax.numpy as jnp
from jax import lax

HID = 1024
CIN = 64
STEPS = 2
NY = 144
NX = 144


def level_of(key, shape, shards, low, largest):
    loudness = 1.0
    for dim, shards_of in shards:
        heights = jax.random.uniform(jax.random.fold_in(jax.random.fold_in(key, 6), dim), (shards_of,), jnp.float32, low / len(shards), largest / len(shards))
        loudness = loudness * jnp.repeat(jnp.exp(heights), shape[dim] // shards_of).reshape((-1,) + (1,) * (len(shape) - 1 - dim))
    return loudness


def gaussian(stream_key, extent, deviation, reach, cuts=(), kind=jnp.bfloat16):
    drawn = jax.random.normal(stream_key, extent, jnp.float32) * deviation
    if len(cuts) > 0:
        drawn = level_of(stream_key, extent, cuts, -0.22, 0.18) * drawn
    return jnp.clip(drawn, min=-reach, max=reach).astype(kind)


def setup_inputs(seed: int = 0) -> dict:
    key_of = jax.random.split(jax.random.key(seed), 7)
    frames = gaussian(key_of[0], (NY, NX, STEPS * CIN), 1.0, 6.0, ((0, 4), (1, 4)))
    w_input = gaussian(key_of[1], (9, CIN, 4, HID), (9 * CIN) ** -0.5, 0.25, ((3, 2),))
    w_hidden = gaussian(key_of[2], (9, HID, 4, HID), (9 * HID) ** -0.5, 0.0625, ((3, 2),))
    biases = gaussian(key_of[3], (4, HID), 1.0, 4.0, ((1, 2),), jnp.float32)
    hidden_init = jnp.clip(jax.random.uniform(key_of[4], (NY, NX, HID), jnp.float32, -1.0, 1.0) * level_of(key_of[4], (NY, NX, HID), ((0, 4), (1, 4), (2, 2)), -0.4, 0.0), -1.0, 1.0).astype(jnp.bfloat16)
    cell_init = gaussian(key_of[5], (NY, NX, HID), 1.0, 5.0, ((0, 4), (1, 4), (2, 2)), jnp.float32)
    return {"frames": frames, "w_input": w_input, "w_hidden": w_hidden, "biases": biases, "hidden_init": hidden_init, "cell_init": cell_init}


def convolve(field, kernels):
    channels = field.shape[-1]
    rhs = kernels.astype(jnp.float32).reshape(3, 3, channels, -1)
    out = lax.conv_general_dilated(field.astype(jnp.float32)[None], rhs, (1, 1), "SAME", dimension_numbers=("NHWC", "HWIO", "NHWC"))
    return out[0]


def reference(frames, w_input, w_hidden, biases, hidden_init, cell_init):
    hidden = hidden_init
    cell = cell_init
    rows, cols = hidden.shape[0], hidden.shape[1]
    for step in range(STEPS):
        frame = frames[:, :, step * CIN:(step + 1) * CIN]
        pre = convolve(frame, w_input) + convolve(hidden, w_hidden)
        pre = pre.reshape(rows, cols, 4, HID) + biases[None, None]
        cell = jax.nn.sigmoid(pre[:, :, 1]) * cell + jax.nn.sigmoid(pre[:, :, 0]) * jnp.tanh(pre[:, :, 3])
        hidden = (jax.nn.sigmoid(pre[:, :, 2]) * jnp.tanh(cell)).astype(jnp.bfloat16)
    return hidden, cell
```

```python
import functools

import jax
import jax.numpy as jnp
from jax import lax
from jax.experimental import pallas as pl
from jax.experimental.pallas import tpu as pltpu
from jax.sharding import PartitionSpec as P

STEPS = 2
LANES = 128
F32 = jnp.float32
BF16 = jnp.bfloat16
VMEM = 60 * 2**20


def up_to(value, multiple):
    return -(-value // multiple) * multiple


def weights_kernel(depth, blocks, w_ref, u_ref, wide_ref):
    for j in range(blocks):
        lanes = slice(LANES * j, LANES * j + LANES)
        for a in range(3):
            wide_ref[a] = w_ref[a, 0, :, :, lanes].astype(F32).reshape(depth * 4, LANES)
        for gate in range(4):
            g0, g1, g2 = [wide_ref[a, pl.ds(gate, depth, stride=4), :] for a in range(3)]
            ends = g0 + g2
            out = slice(LANES * gate, LANES * gate + LANES)
            u_ref[j, 0, 0, :, out] = (ends + g1).astype(BF16)
            u_ref[j, 0, 1, :, out] = (ends - g1).astype(BF16)
            u_ref[j, 1, 0, :, out] = g0.astype(BF16)
            u_ref[j, 1, 1, :, out] = g2.astype(BF16)


def transformed_weights(w_hidden):
    channels, width = w_hidden.shape[1], w_hidden.shape[3]
    blocks = width // LANES
    depth = 256
    steps = channels // depth
    w = w_hidden.reshape(3, 3, channels, 4, width)
    return pl.pallas_call(
        functools.partial(weights_kernel, depth, blocks),
        grid=(3, steps),
        in_specs=[pl.BlockSpec((3, 1, depth, 4, width), lambda b, k: (0, b, k, 0, 0))],
        out_specs=pl.BlockSpec(
            (blocks, 2, 2, depth, 4 * LANES), lambda b, k: (0, 0, 0, b * steps + k, 0)
        ),
        out_shape=jax.ShapeDtypeStruct((blocks, 2, 2, 3 * channels, 4 * LANES), BF16),
        scratch_shapes=[pltpu.VMEM((3, depth * 4, LANES), F32)],
        compiler_params=pltpu.CompilerParams(vmem_limit_bytes=VMEM),
        cost_estimate=pl.CostEstimate(
            flops=0, bytes_accessed=42 * channels * 4 * width, transcendentals=0
        ),
        name="weights",
    )(w)


def sigmoid(x):
    return 0.5 * jnp.tanh(0.5 * x) + 0.5


def step_kernel(dims, offset_ref, *refs):
    stride, height, tiles, parts, last, cols = dims
    hidden_refs, refs = refs[:parts], refs[parts:]
    frame_ref, u_ref, w_ref, bias_ref, cell_ref = refs[:5]
    refs = refs[5:]
    if not last:
        mask_ref, refs = refs[0], refs[1:]
    hidden_out, cell_out, v_ref, x_ref, pre_ref, wide_ref = refs
    channels = v_ref.shape[2] // 3
    half = pl.program_id(1)

    @pl.when((pl.program_id(0) == 0) & (half == 0))
    def _():
        fill = wide_ref.shape[1] - frame_ref.shape[1]
        wide_ref[:, frame_ref.shape[1] :, :] = jnp.zeros((2, fill, LANES), F32)
        wide_ref[:, : frame_ref.shape[1], :] = frame_ref[...].astype(F32)
        for p in range(2):
            for a in range(3):
                for one in range(2):
                    start = stride * ((p + a) // 2) + one
                    at = 256 * a + LANES * one
                    x_ref[p, :, at : at + LANES] = wide_ref[
                        (p + a) % 2, start : start + height, :
                    ].astype(BF16)
        for part, hidden_ref in enumerate(hidden_refs):
            rows = hidden_ref.shape[1]

            @pl.loop(0, hidden_ref.shape[2] // LANES)
            def _(j):
                at = pl.multiple_of(j * LANES, LANES)
                wide_ref[:, :rows, :] = hidden_ref[:, :, pl.ds(at, LANES)].astype(F32)
                for b in range(3):
                    d0 = wide_ref[0, b : b + height, :]
                    d1 = wide_ref[1, b : b + height, :]
                    d2 = wide_ref[0, stride + b : stride + b + height, :]
                    d3 = wide_ref[1, stride + b : stride + b + height, :]
                    to = pl.multiple_of(offset_ref[part] + j * LANES + b * channels, LANES)
                    v_ref[0, :, pl.ds(to, LANES)] = (d0 - d2).astype(BF16)
                    v_ref[1, :, pl.ds(to, LANES)] = (d1 + d2).astype(BF16)
                    v_ref[2, :, pl.ds(to, LANES)] = (d2 - d1).astype(BF16)
                    v_ref[3, :, pl.ds(to, LANES)] = (d1 - d3).astype(BF16)

    def dot(a, b):
        return jnp.dot(a, b, preferred_element_type=F32)

    @pl.when(half == 0)
    def _():
        for low, high in tiles:
            m = slice(low, high)
            plus = dot(v_ref[1, m, :], u_ref[0, 0, 0])
            minus = dot(v_ref[2, m, :], u_ref[0, 0, 1])
            pre_ref[0, m, :] = 0.5 * (plus + minus) + (dot(x_ref[0, m, :], w_ref[0]) + bias_ref[0])
            pre_ref[1, m, :] = 0.5 * (plus - minus) + (dot(x_ref[1, m, :], w_ref[0]) + bias_ref[0])

    @pl.when(half == 1)
    def _():
        for low, high in tiles:
            m = slice(low, high)
            for p in range(2):
                edge = dot(v_ref[3 * p, m, :], u_ref[0, 0, p])
                pre = pre_ref[p, m, :] - edge if p else pre_ref[p, m, :] + edge
                i, f, o, g = [pre[:, LANES * k : LANES * k + LANES] for k in range(4)]
                if last:
                    skip = 1 + stride * p
                    before = cell_ref[0, 1 - p, low + skip : high + skip, :]
                else:
                    before = cell_ref[p, m, :]
                cell = sigmoid(f) * before + sigmoid(i) * jnp.tanh(g)
                hidden = sigmoid(o) * jnp.tanh(cell)
                if last:
                    for t in range(low // stride, high // stride):
                        r = slice(t * stride - low, t * stride - low + cols)
                        cell_out[2 * t + p] = cell[r]
                        hidden_out[2 * t + p] = hidden[r].astype(BF16)
                else:
                    cell_out[0, p, m, :] = cell
                    hidden_out[p, m, :] = jnp.where(mask_ref[p, m, :] > 0, hidden, 0).astype(BF16)


def run_step(offsets, hiddens, frame, u, w_in, bias, cell, mask, stride, pairs, rows, cols):
    last = mask is None
    blocks = u.shape[0]
    channels = u.shape[3] // 3
    height = up_to(pairs * stride, 16)
    cut = stride * 2
    middle = up_to(height // 2, cut) if last else height // 2
    tiles = ((0, middle), (middle, height))
    parts = len(hiddens)
    wide = up_to(max(h.shape[1] for h in hiddens + [frame]), 8)
    wide = up_to(max(wide, height + stride + 2), 8)
    dims = (stride, height, tiles, parts, last, cols)
    once = pl.Buffered(1)
    whole = lambda array: pl.BlockSpec(
        array.shape, lambda n, s: (0,) * array.ndim, pipeline_mode=once
    )
    in_specs = [pl.BlockSpec(memory_space=pltpu.SMEM)]
    in_specs += [whole(h) for h in hiddens]
    in_specs += [
        whole(frame),
        pl.BlockSpec((1, 1, 2, 3 * channels, 4 * LANES), lambda n, s: (n, s, 0, 0, 0)),
        pl.BlockSpec((1, w_in.shape[1], 4 * LANES), lambda n, s: (n, 0, 0)),
        pl.BlockSpec((1, 1, 4 * LANES), lambda n, s: (n, 0, 0)),
    ]
    args = [offsets, *hiddens, frame, u, w_in, bias, cell]
    if last:
        in_specs.append(pl.BlockSpec((1,) + cell.shape[1:], lambda n, s: (n, 0, 0, 0)))
        shape = (rows, cols, blocks * LANES)
        out_specs = (pl.BlockSpec((rows, cols, LANES), lambda n, s: (0, 0, n)),) * 2
        out_shape = (jax.ShapeDtypeStruct(shape, BF16), jax.ShapeDtypeStruct(shape, F32))
    else:
        in_specs.append(pl.BlockSpec((2, height, LANES), lambda n, s: (0, 0, n)))
        in_specs.append(whole(mask))
        args.append(mask)
        out_specs = (
            pl.BlockSpec((2, height, LANES), lambda n, s: (0, 0, n)),
            pl.BlockSpec((1, 2, height, LANES), lambda n, s: (n, 0, 0, 0)),
        )
        out_shape = (
            jax.ShapeDtypeStruct((2, height, blocks * LANES), BF16),
            jax.ShapeDtypeStruct((blocks, 2, height, LANES), F32),
        )
    flops = 2 * height * blocks * 4 * LANES * (12 * channels + 2 * w_in.shape[1])
    return pl.pallas_call(
        functools.partial(step_kernel, dims),
        grid=(blocks, 2),
        in_specs=in_specs,
        out_specs=out_specs,
        out_shape=out_shape,
        scratch_shapes=[
            pltpu.VMEM((4, height, 3 * channels), BF16),
            pltpu.VMEM((2, height, w_in.shape[1]), BF16),
            pltpu.VMEM((2, height, 4 * LANES), F32),
            pltpu.VMEM((2, wide, LANES), F32),
        ],
        compiler_params=pltpu.CompilerParams(vmem_limit_bytes=VMEM),
        cost_estimate=pl.CostEstimate(
            flops=flops, bytes_accessed=u.size * 2, transcendentals=height * blocks * LANES * 10
        ),
        name="step",
    )(*args)


def forward(x, axis):
    count = lax.axis_size(axis)
    return lax.ppermute(x, axis, [(i, i + 1) for i in range(count - 1)])


def backward(x, axis):
    count = lax.axis_size(axis)
    return lax.ppermute(x, axis, [(i + 1, i) for i in range(count - 1)])


def split(x):
    high = lax.reduce_precision(x, 8, 7)
    return high.astype(BF16), (x - high).astype(BF16)


def joined(high, low):
    return high.astype(F32) + low.astype(F32)


def extended(hidden, frames, cell, axis, dim):
    size = hidden.shape[dim]

    def packed(two, one):
        high, low = split(lax.slice_in_dim(cell, one, one + 1, axis=dim))
        ends = jnp.concatenate([high, low], axis=dim)
        taken = [lax.slice_in_dim(a, two, two + 2, axis=dim) for a in (hidden, frames)]
        if dim == 1:
            extra = hidden.shape[0] - cell.shape[0]
            ends = jnp.pad(ends, ((0, extra), (0, 0), (0, 0)))
        return jnp.concatenate(taken + [ends], axis=2)

    before = forward(packed(size - 2, cell.shape[dim] - 1), axis)
    after = backward(packed(0, 0), axis)
    first, second = hidden.shape[2], hidden.shape[2] + frames.shape[2]

    def one(got):
        ends = got[: cell.shape[0], :, second:] if dim == 1 else got[:, :, second:]
        high = lax.slice_in_dim(ends, 0, 1, axis=dim)
        low = lax.slice_in_dim(ends, 1, 2, axis=dim)
        return joined(high, low)

    return (
        jnp.concatenate([before[:, :, :first], hidden, after[:, :, :first]], axis=dim),
        jnp.concatenate(
            [before[:, :, first:second], frames, after[:, :, first:second]], axis=dim
        ),
        jnp.concatenate([one(before), cell, one(after)], axis=dim),
    )


def planes(x, stride):
    rows, cols, channels = x.shape
    x = jnp.pad(x, ((0, 0), (0, stride - cols), (0, 0)))
    x = x.reshape(rows // 2, 2, stride, channels).transpose(1, 0, 2, 3)
    return x.reshape(2, rows // 2 * stride, channels)


def frame_planes(frame, stride):
    beside = jnp.pad(frame[:, 1:], ((0, 0), (0, 1), (0, 0)))
    return planes(jnp.concatenate([frame, beside], axis=2), stride)


def gathered(hidden):
    count = lax.axis_size("ch")
    width = hidden.shape[2]
    if count == 2:
        other = lax.ppermute(hidden, "ch", [(0, 1), (1, 0)])
        me = lax.axis_index("ch")
        return [hidden, other], jnp.stack([me * width, (1 - me) * width]).astype(jnp.int32)
    every = lax.all_gather(hidden, "ch")
    return [every[i] for i in range(count)], jnp.arange(count, dtype=jnp.int32) * width


def input_weights(w_input):
    _, depth, _, width = w_input.shape
    w = w_input.reshape(3, 3, depth, 4, width // LANES, LANES)
    w = jnp.stack([w[:, 0], w[:, 1], jnp.zeros_like(w[:, 1]), w[:, 2]], axis=1)
    return w.transpose(4, 0, 1, 2, 3, 5).reshape(width // LANES, 12 * depth, 4 * LANES)


def inside(rows, cols, stride, height):
    p = lax.broadcasted_iota(jnp.int32, (2, height, LANES), 0)
    flat = lax.broadcasted_iota(jnp.int32, (2, height, LANES), 1)
    y = 2 * (flat // stride) + p - 1 + lax.axis_index("sy") * rows
    x = flat % stride - 1
    wholly = (x <= cols) & (flat // stride <= rows // 2)
    x = x + lax.axis_index("sx") * cols
    ny, nx = rows * lax.axis_size("sy"), cols * lax.axis_size("sx")
    return ((y >= 0) & (y < ny) & (x >= 0) & (x < nx) & wholly).astype(F32)


def per_device(frames, w_input, w_hidden, biases, hidden_init, cell_init):
    rows, cols, width = hidden_init.shape
    stride = up_to(cols + 4, 8)
    half = frames.shape[2] // STEPS
    blocks = width // LANES
    u = transformed_weights(w_hidden)
    w_in = input_weights(w_input)
    bias = biases.reshape(4, blocks, LANES).transpose(1, 0, 2).reshape(blocks, 1, 4 * LANES)
    wider = extended(hidden_init, frames, cell_init, "sy", 0)
    hidden, framed, cell = extended(*wider, "sx", 1)
    hiddens, offsets = gathered(planes(hidden, stride))
    height = up_to((rows // 2 + 1) * stride, 16)
    cell = planes(cell, stride)
    cell = jnp.pad(cell, ((0, 0), (0, height - cell.shape[1]), (0, 0)))
    mask = inside(rows, cols, stride, height)
    frame = frame_planes(framed[:, :, :half], stride)
    hidden, cell = run_step(
        offsets, hiddens, frame, u, w_in, bias, cell, mask, stride, rows // 2 + 1, rows, cols
    )
    hiddens, offsets = gathered(hidden)
    frame = frame_planes(framed[1:-1, 1:-1, half:], stride)
    return run_step(
        offsets, hiddens, frame, u, w_in, bias, cell, None, stride, rows // 2, rows, cols
    )


def solution(mesh):
    in_specs = (
        P("sy", "sx", None),
        P(None, None, None, "ch"),
        P(None, None, None, "ch"),
        P(None, "ch"),
        P("sy", "sx", "ch"),
        P("sy", "sx", "ch"),
    )
    out_specs = (P("sy", "sx", "ch"), P("sy", "sx", "ch"))
    return jax.shard_map(
        per_device, mesh=mesh, in_specs=in_specs, out_specs=out_specs, check_vma=False
    )
```

```python
import functools

import jax
import jax.numpy as jnp
from jax import lax
from jax.experimental import pallas as pl
from jax.experimental.pallas import tpu as pltpu
from jax.sharding import PartitionSpec as P

STEPS = 2
LANES = 128
GATES = 4 * LANES
F32 = jnp.float32
BF16 = jnp.bfloat16
VMEM = 60 * 2**20


def up_to(value, multiple):
    return -(-value // multiple) * multiple


def params():
    return pltpu.CompilerParams(vmem_limit_bytes=VMEM)


def input_weights_kernel(depth, blocks, w_ref, *refs):
    out_ref, wide_ref = refs[-2:]
    for j in range(blocks):
        lanes = slice(LANES * j, LANES * j + LANES)
        for b in range(3):
            wide_ref[b] = w_ref[0, b, :, :, lanes].astype(F32).reshape(depth * 4, LANES)
        for gate in range(4):
            out = slice(LANES * gate, LANES * gate + LANES)
            for b in range(3):
                rows = wide_ref[b, pl.ds(gate, depth, stride=4), :]
                out_ref[j, depth * b : depth * b + depth, out] = rows.astype(BF16)
        out_ref[j, 3 * depth :, :] = jnp.zeros((depth, GATES), BF16)


def input_weights(w_input, *after):
    _, depth, _, width = w_input.shape
    blocks = width // LANES
    return pl.pallas_call(
        functools.partial(input_weights_kernel, depth, blocks),
        grid=(3,),
        in_specs=[pl.BlockSpec((1, 3, depth, 4, width), lambda a: (a, 0, 0, 0, 0))]
        + [pl.BlockSpec(memory_space=pl.ANY)] * len(after),
        out_specs=pl.BlockSpec((blocks, 4 * depth, GATES), lambda a: (0, a, 0)),
        out_shape=jax.ShapeDtypeStruct((blocks, 12 * depth, GATES), BF16),
        scratch_shapes=[pltpu.VMEM((3, depth * 4, LANES), F32)],
        compiler_params=params(),
        cost_estimate=pl.CostEstimate(
            flops=0, bytes_accessed=48 * depth * 4 * width, transcendentals=0
        ),
        name="input_weights",
    )(w_input.reshape(3, 3, depth, 4, width), *after)


def sigmoid(x):
    return 0.5 * jnp.tanh(0.5 * x) + 0.5


def place(out_ref, origin, sizes, inner, rim_row, rim_col):
    rows, cols, stride = sizes
    for y in range(-origin, rows + origin):
        at = y + origin
        start = stride * (at // 2) + origin
        if y < 0:
            row = rim_row(0, y + 2)
        elif y >= rows:
            row = rim_row(1, y - rows)
        else:
            row = inner(y)
        out_ref[at % 2, start : start + cols, :] = row
    pairs = rows // 2 + origin
    for p in range(2):
        skip = (p + 2 - origin) // 2
        for k in range(origin):
            left = rim_col(0, 2 - origin + k, (p - origin) % 2)
            right = rim_col(1, k, (p - origin) % 2)
            out_ref[p, pl.ds(k, pairs, stride=stride), :] = left[skip : skip + pairs]
            at = origin + cols + k
            out_ref[p, pl.ds(at, pairs, stride=stride), :] = right[skip : skip + pairs]


def pass_kernel(dims, *refs):
    sizes, height, tiles, step, raw, first, final, into = dims
    rows, cols, stride = sizes
    fused = step == 0
    key_ref, refs = refs[0], list(refs[1:])
    take = lambda count: [refs.pop(0) for _ in range(count)]
    hidden_refs = take(3 if raw else 1)
    if first:
        frame_ref, frame_rows_ref, frame_cols_ref, w_ref, bias_ref = take(5)
    else:
        (before_ref,) = take(1)
    (u_ref,) = take(1)
    if fused:
        raw_ref = u_ref
        take(into)
    if final and step == 0:
        cell_in_ref, cell_rows_ref, cell_cols_ref, mask_ref = take(4)
    elif final:
        (cell_ref,) = take(1)
    if final:
        hidden_out, cell_out = take(2)
    else:
        (pre_ref,) = take(1)
    if fused:
        (u_ref,) = take(1)
    v_ref, wide_ref = take(2)
    if first:
        (x_ref,) = take(1)
    if final:
        (pre_ref,) = take(1)
    if final and step == 0:
        (cell_ref,) = take(1)
    if fused:
        (flat_ref,) = take(1)
    channels = v_ref.shape[2] // 3

    def build_x():
        inner = lambda y: frame_ref[y].astype(F32)
        rim_row = lambda side, k: frame_rows_ref[2 * side + k]
        rim_col = lambda side, k, p: frame_cols_ref[4 * side + 2 * k + p]
        place(wide_ref, 2 - step, sizes, inner, rim_row, rim_col)
        chunk = 48 if height % 48 == 0 else 16
        low = lax.broadcasted_iota(jnp.int32, (chunk, LANES), 1) < LANES // 2
        for q in range(2):
            for pair in range(2):
                for r in range(0, height, chunk):
                    start = stride * pair + r
                    at = [wide_ref[q, start + b : start + b + chunk, :] for b in range(3)]
                    turned = [pltpu.roll(value, LANES // 2, 1) for value in at]
                    if step == 0:
                        two, one = jnp.where(low, at[0], turned[1]), at[2]
                    else:
                        two, one = jnp.where(low, turned[0], at[1]), turned[2]
                    two, one = two.astype(BF16), one.astype(BF16)
                    rows = slice(r, r + chunk)
                    for p in range(2):
                        a = 2 * pair + q - p
                        if 0 <= a < 3:
                            x_ref[p, rows, 256 * a : 256 * a + LANES] = two
                            x_ref[p, rows, 256 * a + LANES : 256 * a + 256] = one

    def build_v(b, to):
        chunk = 48 if height % 48 == 0 else 16
        to = pl.ds(to, LANES)
        for r in range(0, height, chunk):
            near, far = slice(b + r, b + r + chunk), slice(stride + b + r, stride + b + r + chunk)
            d0, d1 = wide_ref[0, near, :], wide_ref[1, near, :]
            d2, d3 = wide_ref[0, far, :], wide_ref[1, far, :]
            rows = slice(r, r + chunk)
            v_ref[0, rows, to] = (d0 - d2).astype(BF16)
            v_ref[1, rows, to] = (d1 + d2).astype(BF16)
            v_ref[2, rows, to] = (d2 - d1).astype(BF16)
            v_ref[3, rows, to] = (d1 - d3).astype(BF16)

    def transform(b, c, chunk):
        rows = slice(c, c + chunk)
        for a in range(3):
            taken = raw_ref[a, b, rows, :, :].astype(F32)
            flat_ref[a, 4 * c : 4 * (c + chunk), :] = taken.reshape(4 * chunk, LANES)
        for gate in range(4):
            at = pl.ds(4 * c + gate, chunk, stride=4)
            g0, g1, g2 = [flat_ref[a, at, :] for a in range(3)]
            ends = g0 + g2
            out = slice(LANES * gate, LANES * gate + LANES)
            u_ref[0, 0, 0, b, rows, out] = (ends + g1).astype(BF16)
            u_ref[0, 0, 1, b, rows, out] = (ends - g1).astype(BF16)
            u_ref[0, 1, 0, b, rows, out] = g0.astype(BF16)
            u_ref[0, 1, 1, b, rows, out] = g2.astype(BF16)

    @pl.when(pl.program_id(0) == 0)
    def _():
        wide_ref[...] = jnp.zeros(wide_ref.shape, F32)
        if first:
            build_x()

        @pl.loop(0, channels // LANES)
        def _(j):
            lanes = pl.ds(pl.multiple_of(j * LANES, LANES), LANES)
            if raw:
                inner_ref, rows_ref, cols_ref = hidden_refs
                inner = lambda y: inner_ref[y, :, lanes].astype(F32)
                rim_row = lambda side, k: rows_ref[2 * side + k, :, lanes]
                rim_col = lambda side, k, p: cols_ref[4 * side + 2 * k + p, :, lanes]
                place(wide_ref, 2, sizes, inner, rim_row, rim_col)
            else:
                (hidden_ref,) = hidden_refs
                wide_ref[:, : hidden_ref.shape[1], :] = hidden_ref[:, :, lanes].astype(F32)
            for b in range(3):
                build_v(b, pl.multiple_of(b * channels + j * LANES, LANES))

    if final and step == 0:
        cell_ref[0] = jnp.zeros(cell_ref.shape[1:], F32)
        place(
            cell_ref.at[0],
            1,
            sizes,
            lambda y: cell_in_ref[y],
            lambda side, k: cell_rows_ref[2 * side] + cell_rows_ref[2 * side + 1],
            lambda side, k, p: cell_cols_ref[4 * side + p] + cell_cols_ref[4 * side + 2 + p],
        )

    def dot(a, b):
        return jnp.dot(a, b, preferred_element_type=F32)

    def gates(low, high, p, pre):
        m = slice(low, high)
        i, f, o, g = [pre[:, LANES * k : LANES * k + LANES] for k in range(4)]
        if step == 0:
            before = cell_ref[0, p, m, :]
        else:
            skip = 1 + stride * p
            before = cell_ref[0, 1 - p, low + skip : high + skip, :]
        cell = sigmoid(f) * before + sigmoid(i) * jnp.tanh(g)
        hidden = sigmoid(o) * jnp.tanh(cell)
        if step == 0:
            cell_out[0, p, m, :] = cell
            hidden_out[p, m, :] = jnp.where(mask_ref[p, m, :] > 0, hidden, 0).astype(BF16)
        else:
            for t in range(low // stride, high // stride):
                r = slice(t * stride - low, t * stride - low + cols)
                cell_out[2 * t + p] = cell[r]
                hidden_out[2 * t + p] = hidden[r].astype(BF16)

    chunk = 32
    groups = 3 if fused else 1
    depth = 3 * channels // groups
    if fused:
        for c in range(0, channels, chunk):
            transform(0, c, chunk)
    for group in range(groups):
        ready = group * depth
        waiting = []
        if fused and group < 2:
            waiting = [(group + 1, c, chunk) for c in range(0, channels, chunk)]
        share = -(-len(waiting) // (4 * len(tiles)))
        for low, high in tiles:
            m = slice(low, high)
            made = {}
            for k in (1, 2, 0, 3):
                place_of = {1: (0, 0), 2: (0, 1), 0: (1, 0), 3: (1, 1)}[k]
                if fused:
                    weights = u_ref[0, place_of[0], place_of[1], group]
                else:
                    weights = u_ref[0, place_of[0], place_of[1]].reshape(depth, GATES)
                made[k] = dot(v_ref[k, m, ready : ready + depth], weights)
                for _ in range(share):
                    if waiting:
                        transform(*waiting.pop(0))
            for p in range(2):
                if group > 0:
                    other = pre_ref[0, p, m, :]
                elif first:
                    bias = jnp.concatenate([bias_ref[k : k + 1, :] for k in range(4)], axis=1)
                    other = dot(x_ref[p, m, :], w_ref[0]) + bias
                else:
                    other = before_ref[0, p, m, :]
                both = made[1] - made[2] if p else made[1] + made[2]
                edge = -made[3] if p else made[0]
                pre = 0.5 * both + edge + other
                if final and group == groups - 1:
                    gates(low, high, p, pre)
                else:
                    pre_ref[0, p, m, :] = pre


def run_pass(step, sizes, half, hidden, u, frame=None, before=None, cell=None, mask=None, into=None):
    rows, cols, stride = sizes
    raw = isinstance(hidden, tuple)
    hiddens = hidden if raw else (hidden,)
    channels = hiddens[0].shape[2]
    first, final, fused = frame is not None, cell is not None, step == 0
    count = u.shape[4] // LANES if fused else u.shape[0]
    pairs = rows // 2 + (1 - step)
    height = up_to(pairs * stride, 16)
    middle = up_to(height // 2, 2 * stride if step else 16)
    tiles = ((0, middle), (middle, height))
    wide = up_to(max((rows // 2 + 2) * stride, height + stride + 2), 8)
    dims = (sizes, height, tiles, step, raw, first, final, int(into is not None))
    once = pl.Buffered(1)

    def whole(array):
        zeros = (0,) * array.ndim
        return pl.BlockSpec(array.shape, lambda n, k: zeros, pipeline_mode=once)

    def add(array, spec=None):
        args.append(array)
        in_specs.append(whole(array) if spec is None else spec)

    args, in_specs, aliases = [], [], {}
    for array in hiddens:
        add(array)
    if first:
        inner, rim_rows, rim_cols, w_in, biases = frame
        add(inner)
        add(rim_rows)
        add(rim_cols)
        add(w_in, pl.BlockSpec((1, w_in.shape[1], GATES), lambda n, k: (n, 0, 0)))
        add(biases, pl.BlockSpec((4, LANES), lambda n, k: (0, n)))
    else:
        add(before, pl.BlockSpec((1, 2, height, GATES), lambda n, k: (n, 0, 0, 0)))
    u_spec = pl.BlockSpec((1, 2, 2, 3, channels, GATES), lambda n, k: (n, 0, 0, 0, k[0], 0))
    if fused:
        add(u, pl.BlockSpec((3, 3, channels, 4, LANES), lambda n, k: (0, 0, k[0], 0, n)))
        if into is not None:
            aliases = {1 + len(args): 2 if final else 1}
            add(into, pl.BlockSpec(memory_space=pl.ANY))
    else:
        add(u, u_spec)
    if final and step == 0:
        for array in cell:
            add(array, pl.BlockSpec(array.shape[:2] + (LANES,), lambda n, k: (0, 0, n)))
        add(mask)
    elif final:
        add(cell, pl.BlockSpec((1,) + cell.shape[1:], lambda n, k: (n, 0, 0, 0)))
    scratch = [
        pltpu.VMEM((4, height, 3 * channels), BF16),
        pltpu.VMEM((2, wide, LANES), F32),
    ]
    if first:
        scratch.append(pltpu.VMEM((2, height, 6 * LANES), BF16))
    if final:
        scratch.append(pltpu.VMEM((1, 2, height, GATES), F32))
    if final and step == 0:
        scratch.append(pltpu.VMEM((1, 2, height, LANES), F32))
    if fused:
        scratch.append(pltpu.VMEM((3, 4 * channels, LANES), F32))
    if not final:
        out_specs = [pl.BlockSpec((1, 2, height, GATES), lambda n, k: (n, 0, 0, 0))]
        out_shape = [jax.ShapeDtypeStruct((count, 2, height, GATES), F32)]
    elif step == 0:
        out_specs = [
            pl.BlockSpec((2, height, LANES), lambda n, k: (0, 0, n)),
            pl.BlockSpec((1, 2, height, LANES), lambda n, k: (n, 0, 0, 0)),
        ]
        out_shape = [
            jax.ShapeDtypeStruct((2, height, count * LANES), BF16),
            jax.ShapeDtypeStruct((count, 2, height, LANES), F32),
        ]
    else:
        shape = (rows, cols, count * LANES)
        out_specs = [pl.BlockSpec((rows, cols, LANES), lambda n, k: (0, 0, n))] * 2
        out_shape = [jax.ShapeDtypeStruct(shape, BF16), jax.ShapeDtypeStruct(shape, F32)]
    if fused:
        out_specs.append(u_spec)
        out_shape.append(jax.ShapeDtypeStruct((count, 2, 2, 3, 2 * channels, GATES), BF16))
    return pl.pallas_call(
        functools.partial(pass_kernel, dims),
        grid_spec=pltpu.PrefetchScalarGridSpec(
            num_scalar_prefetch=1,
            grid=(count,),
            in_specs=in_specs,
            out_specs=out_specs,
            scratch_shapes=scratch,
        ),
        out_shape=out_shape,
        input_output_aliases=aliases,
        compiler_params=params(),
        cost_estimate=pl.CostEstimate(
            flops=2 * height * count * GATES * 12 * channels,
            bytes_accessed=24 * channels * count * GATES,
            transcendentals=height * count * LANES * 10,
        ),
        name="step%d" % step,
    )(half.reshape(1), *args)


def forward(x, axis):
    count = lax.axis_size(axis)
    return lax.ppermute(x, axis, [(i, i + 1) for i in range(count - 1)])


def backward(x, axis):
    count = lax.axis_size(axis)
    return lax.ppermute(x, axis, [(i + 1, i) for i in range(count - 1)])


def swapped(x):
    return lax.ppermute(x, "ch", [(0, 1), (1, 0)])


def split(x):
    high = lax.reduce_precision(x, 8, 7)
    return high.astype(BF16), (x - high).astype(BF16)


def row_pack(hidden, frames, cell, two, one):
    ends = jnp.stack(split(cell[one]))
    return jnp.concatenate([hidden[two : two + 2], frames[two : two + 2], ends], axis=2)


def col_pack(hidden, frames, cell, north, south, two, one):
    rows, _, width = hidden.shape
    main = width + frames.shape[2]
    ends = jnp.stack(split(cell[:, one]), axis=1)
    middle = jnp.concatenate([hidden[:, two : two + 2], frames[:, two : two + 2], ends], axis=2)
    none = jnp.zeros((1, 2, width), BF16)
    upper = jnp.concatenate([none, north[None, :, one, main:]], axis=0)
    lower = jnp.concatenate([south[None, :, one, main:], none], axis=0)
    upper = jnp.concatenate([north[:, two : two + 2, :main], upper], axis=2)
    lower = jnp.concatenate([south[:, two : two + 2, :main], lower], axis=2)
    strip = jnp.concatenate([upper, middle, lower], axis=0)
    strip = strip.reshape(rows // 2 + 2, 2, 2, -1).transpose(2, 1, 0, 3)
    return strip.reshape(4, rows // 2 + 2, -1)


def inside(rows, cols, stride, height):
    p = lax.broadcasted_iota(jnp.int32, (2, height, LANES), 0)
    flat = lax.broadcasted_iota(jnp.int32, (2, height, LANES), 1)
    y = 2 * (flat // stride) + p - 1 + lax.axis_index("sy") * rows
    x = flat % stride - 1
    wholly = (x <= cols) & (flat // stride <= rows // 2)
    x = x + lax.axis_index("sx") * cols
    ny, nx = rows * lax.axis_size("sy"), cols * lax.axis_size("sx")
    return ((y >= 0) & (y < ny) & (x >= 0) & (x < nx) & wholly).astype(F32)


def per_device(frames, w_input, w_hidden, biases, hidden_init, cell_init):
    rows, cols, width = hidden_init.shape
    main = width + frames.shape[2]
    stride = up_to(cols + 4, 8)
    sizes = (rows, cols, stride)
    count = lax.axis_size("ch")
    paired = count == 2
    gather = lambda x: lax.all_gather(x, "ch", axis=x.ndim - 1, tiled=True)
    other = swapped(hidden_init) if paired else gather(hidden_init)
    local = (hidden_init, frames, cell_init)
    to_south = row_pack(*local, rows - 2, rows - 1)
    to_north = row_pack(*local, 0, 0)
    north, south = forward(to_south, "sy"), backward(to_north, "sy")
    w_in = input_weights(w_input, to_south, to_north)
    to_east = col_pack(*local, north, south, cols - 2, cols - 1)
    to_west = col_pack(*local, north, south, 0, 0)
    west, east = forward(to_east, "sx"), backward(to_west, "sx")
    rim_rows, rim_cols = jnp.concatenate([north, south]), jnp.concatenate([west, east])
    length = rim_rows.shape[0] * rim_rows.shape[1]
    ring = jnp.concatenate(
        [rim_rows[:, :, :width].reshape(length, width), rim_cols[:, :, :width].reshape(-1, width)]
    )

    def unpacked(ring):
        ring = ring.astype(F32)
        return (
            ring[:length].reshape(rim_rows.shape[:2] + ring.shape[1:]),
            ring[length:].reshape(rim_cols.shape[:2] + ring.shape[1:]),
        )

    frame = (
        frames,
        rim_rows[:, :, width:main].astype(F32),
        rim_cols[:, :, width:main].astype(F32),
        w_in,
        biases,
    )
    cell = (cell_init, rim_rows[:, :, main:].astype(F32), rim_cols[:, :, main:].astype(F32))
    mask = inside(rows, cols, stride, up_to((rows // 2 + 1) * stride, 16))
    raw = (hidden_init,) + unpacked(ring)
    if paired:
        me = lax.axis_index("ch").astype(jnp.int32)
        halves = (me, 1 - me)
        hiddens = (raw, (other,) + unpacked(swapped(ring)))
    else:
        halves = (jnp.int32(0), jnp.int32(1))
        full = (other,) + unpacked(gather(ring))
        cut = other.shape[2] // 2
        hiddens = [tuple(x[:, :, k * cut : k * cut + cut] for x in full) for k in range(2)]
    w = w_hidden.reshape((3, 3) + w_hidden.shape[1:])
    before, u = run_pass(0, sizes, halves[0], hiddens[0], w, frame=frame)
    hidden, cell, u = run_pass(
        0, sizes, halves[1], hiddens[1], w, before=before, cell=cell, mask=mask, into=u
    )
    if paired:
        hiddens = (hidden, swapped(hidden))
    else:
        full = gather(hidden)
        hiddens = [full[:, :, k * cut : k * cut + cut] for k in range(2)]
    (before,) = run_pass(1, sizes, halves[0], hiddens[0], u, frame=frame)
    return tuple(run_pass(1, sizes, halves[1], hiddens[1], u, before=before, cell=cell))


def solution(mesh):
    in_specs = (
        P("sy", "sx", None),
        P(None, None, None, "ch"),
        P(None, None, None, "ch"),
        P(None, "ch"),
        P("sy", "sx", "ch"),
        P("sy", "sx", "ch"),
    )
    out_specs = (P("sy", "sx", "ch"), P("sy", "sx", "ch"))
    return jax.shard_map(
        per_device, mesh=mesh, in_specs=in_specs, out_specs=out_specs, check_vma=False
    )
```

```python
import functools

import jax
import jax.numpy as jnp
from jax import lax
from jax.experimental import pallas as pl
from jax.experimental.pallas import tpu as pltpu
from jax.sharding import PartitionSpec as P

STEPS = 2
LANES = 128
GATES = 4 * LANES
F32 = jnp.float32
BF16 = jnp.bfloat16
VMEM = 60 * 2**20


def up_to(value, multiple):
    return -(-value // multiple) * multiple


def params():
    return pltpu.CompilerParams(vmem_limit_bytes=VMEM)


def input_weights_kernel(depth, blocks, w_ref, *refs):
    out_ref, wide_ref = refs[-2:]
    for j in range(blocks):
        lanes = slice(LANES * j, LANES * j + LANES)
        for b in range(3):
            wide_ref[b] = w_ref[0, b, :, :, lanes].astype(F32).reshape(depth * 4, LANES)
        for gate in range(4):
            out = slice(LANES * gate, LANES * gate + LANES)
            for b in range(3):
                rows = wide_ref[b, pl.ds(gate, depth, stride=4), :]
                out_ref[j, depth * b : depth * b + depth, out] = rows.astype(BF16)
        out_ref[j, 3 * depth :, :] = jnp.zeros((depth, GATES), BF16)


def input_weights(w_input, *after):
    _, depth, _, width = w_input.shape
    blocks = width // LANES
    return pl.pallas_call(
        functools.partial(input_weights_kernel, depth, blocks),
        grid=(3,),
        in_specs=[pl.BlockSpec((1, 3, depth, 4, width), lambda a: (a, 0, 0, 0, 0))]
        + [pl.BlockSpec(memory_space=pl.ANY)] * len(after),
        out_specs=pl.BlockSpec((blocks, 4 * depth, GATES), lambda a: (0, a, 0)),
        out_shape=jax.ShapeDtypeStruct((blocks, 12 * depth, GATES), BF16),
        scratch_shapes=[pltpu.VMEM((3, depth * 4, LANES), F32)],
        compiler_params=params(),
        cost_estimate=pl.CostEstimate(
            flops=0, bytes_accessed=48 * depth * 4 * width, transcendentals=0
        ),
        name="input_weights",
    )(w_input.reshape(3, 3, depth, 4, width), *after)


def sigmoid(x):
    return 0.5 * jnp.tanh(0.5 * x) + 0.5


def place(out_ref, origin, sizes, inner, rim_row, rim_col):
    rows, cols, stride = sizes
    for y in range(-origin, rows + origin):
        at = y + origin
        start = stride * (at // 2) + origin
        if y < 0:
            row = rim_row(0, y + 2)
        elif y >= rows:
            row = rim_row(1, y - rows)
        else:
            row = inner(y)
        out_ref[at % 2, start : start + cols, :] = row
    pairs = rows // 2 + origin
    for p in range(2):
        skip = (p + 2 - origin) // 2
        for k in range(origin):
            left = rim_col(0, 2 - origin + k, (p - origin) % 2)
            right = rim_col(1, k, (p - origin) % 2)
            out_ref[p, pl.ds(k, pairs, stride=stride), :] = left[skip : skip + pairs]
            at = origin + cols + k
            out_ref[p, pl.ds(at, pairs, stride=stride), :] = right[skip : skip + pairs]


def pass_kernel(dims, *refs):
    sizes, height, tiles, step, raw, first, final, into = dims
    rows, cols, stride = sizes
    fused = step == 0
    key_ref, refs = refs[0], list(refs[1:])
    take = lambda count: [refs.pop(0) for _ in range(count)]
    hidden_refs = take(5 if raw else 1)
    if first:
        frame_refs = take(5)
        w_ref, bias_ref = take(2)
    else:
        (before_ref,) = take(1)
    (u_ref,) = take(1)
    if fused:
        raw_ref = u_ref
        take(into)
    if final and step == 0:
        cell_refs = take(5)
    elif final:
        (cell_ref,) = take(1)
    if final:
        hidden_out, cell_out = take(2)
    else:
        (pre_ref,) = take(1)
    if fused:
        (u_ref,) = take(1)
    v_ref, wide_ref = take(2)
    if first:
        (x_ref,) = take(1)
    if final:
        (pre_ref,) = take(1)
    if final and step == 0:
        cell_ref, mask_ref = take(2)
    if fused:
        (flat_ref,) = take(1)
    channels = v_ref.shape[2] // 3

    def surrounded(tile_refs, lanes):
        inner_ref, rows_refs, cols_refs = tile_refs[0], tile_refs[1:3], tile_refs[3:5]
        return (
            lambda y: inner_ref[y, :, lanes].astype(F32),
            lambda side, k: rows_refs[side][k, :, lanes].astype(F32),
            lambda side, k, p: cols_refs[side][2 * k + p, :, lanes].astype(F32),
        )

    def build_x():
        place(wide_ref, 2 - step, sizes, *surrounded(frame_refs, slice(None)))
        chunk = 48 if height % 48 == 0 else 16
        low = lax.broadcasted_iota(jnp.int32, (chunk, LANES), 1) < LANES // 2
        for q in range(2):
            for pair in range(2):
                for r in range(0, height, chunk):
                    start = stride * pair + r
                    at = [wide_ref[q, start + b : start + b + chunk, :] for b in range(3)]
                    turned = [pltpu.roll(value, LANES // 2, 1) for value in at]
                    if step == 0:
                        two, one = jnp.where(low, at[0], turned[1]), at[2]
                    else:
                        two, one = jnp.where(low, turned[0], at[1]), turned[2]
                    two, one = two.astype(BF16), one.astype(BF16)
                    rows = slice(r, r + chunk)
                    for p in range(2):
                        a = 2 * pair + q - p
                        if 0 <= a < 3:
                            x_ref[p, rows, 256 * a : 256 * a + LANES] = two
                            x_ref[p, rows, 256 * a + LANES : 256 * a + 256] = one

    def build_v(b, to):
        chunk = 48 if height % 48 == 0 else 16
        to = pl.ds(to, LANES)
        for r in range(0, height, chunk):
            near, far = slice(b + r, b + r + chunk), slice(stride + b + r, stride + b + r + chunk)
            d0, d1 = wide_ref[0, near, :], wide_ref[1, near, :]
            d2, d3 = wide_ref[0, far, :], wide_ref[1, far, :]
            rows = slice(r, r + chunk)
            v_ref[0, rows, to] = (d0 - d2).astype(BF16)
            v_ref[1, rows, to] = (d1 + d2).astype(BF16)
            v_ref[2, rows, to] = (d2 - d1).astype(BF16)
            v_ref[3, rows, to] = (d1 - d3).astype(BF16)

    def transform(b, c, chunk):
        rows = slice(c, c + chunk)
        for a in range(3):
            taken = raw_ref[a, b, rows, :, :].astype(F32)
            flat_ref[a, 4 * c : 4 * (c + chunk), :] = taken.reshape(4 * chunk, LANES)
        for gate in range(4):
            at = pl.ds(4 * c + gate, chunk, stride=4)
            g0, g1, g2 = [flat_ref[a, at, :] for a in range(3)]
            ends = g0 + g2
            out = slice(LANES * gate, LANES * gate + LANES)
            u_ref[0, 0, 0, b, rows, out] = (ends + g1).astype(BF16)
            u_ref[0, 0, 1, b, rows, out] = (ends - g1).astype(BF16)
            u_ref[0, 1, 0, b, rows, out] = g0.astype(BF16)
            u_ref[0, 1, 1, b, rows, out] = g2.astype(BF16)

    @pl.when(pl.program_id(0) == 0)
    def _():
        wide_ref[...] = jnp.zeros(wide_ref.shape, F32)
        if first:
            build_x()

        @pl.loop(0, channels // LANES)
        def _(j):
            lanes = pl.ds(pl.multiple_of(j * LANES, LANES), LANES)
            if raw:
                place(wide_ref, 2, sizes, *surrounded(hidden_refs, lanes))
            else:
                (hidden_ref,) = hidden_refs
                wide_ref[:, : hidden_ref.shape[1], :] = hidden_ref[:, :, lanes].astype(F32)
            for b in range(3):
                build_v(b, pl.multiple_of(b * channels + j * LANES, LANES))

        if final and step == 0:
            mask_ref[...] = jnp.zeros(mask_ref.shape, F32)
            edge = lambda k, length: jnp.where(key_ref[2 + k] > 0, jnp.ones((length, LANES), F32), 0)
            place(
                mask_ref,
                1,
                sizes,
                lambda y: jnp.ones((cols, LANES), F32),
                lambda side, k: edge(side, cols),
                lambda side, k, p: edge(2 + side, rows // 2 + 2),
            )
            low, high = slice(0, stride), slice(rows // 2 * stride, rows // 2 * stride + stride)
            mask_ref[0, low, :] = jnp.where(key_ref[2] > 0, mask_ref[0, low, :], 0)
            mask_ref[1, high, :] = jnp.where(key_ref[3] > 0, mask_ref[1, high, :], 0)

    if final and step == 0:
        cell_ref[0] = jnp.zeros(cell_ref.shape[1:], F32)
        inner, rim_row, rim_col = surrounded(cell_refs, slice(None))
        place(
            cell_ref.at[0],
            1,
            sizes,
            inner,
            lambda side, k: rim_row(side, 0) + rim_row(side, 1),
            lambda side, k, p: rim_col(side, 0, p) + rim_col(side, 1, p),
        )

    def dot(a, b):
        return jnp.dot(a, b, preferred_element_type=F32)

    def gates(low, high, p, pre):
        m = slice(low, high)
        i, f, o, g = [pre[:, LANES * k : LANES * k + LANES] for k in range(4)]
        if step == 0:
            before = cell_ref[0, p, m, :]
        else:
            skip = 1 + stride * p
            before = cell_ref[0, 1 - p, low + skip : high + skip, :]
        cell = sigmoid(f) * before + sigmoid(i) * jnp.tanh(g)
        hidden = sigmoid(o) * jnp.tanh(cell)
        if step == 0:
            cell_out[0, p, m, :] = cell
            hidden_out[p, m, :] = jnp.where(mask_ref[p, m, :] > 0, hidden, 0).astype(BF16)
        else:
            for t in range(low // stride, high // stride):
                r = slice(t * stride - low, t * stride - low + cols)
                cell_out[2 * t + p] = cell[r]
                hidden_out[2 * t + p] = hidden[r].astype(BF16)

    chunk = 32
    groups = 3 if fused else 1
    depth = 3 * channels // groups
    if fused:
        for c in range(0, channels, chunk):
            transform(0, c, chunk)
    for group in range(groups):
        ready = group * depth
        waiting = []
        if fused and group < 2:
            waiting = [(group + 1, c, chunk) for c in range(0, channels, chunk)]
        share = -(-len(waiting) // (4 * len(tiles)))
        for low, high in tiles:
            m = slice(low, high)
            made = {}
            for k in (1, 2, 0, 3):
                place_of = {1: (0, 0), 2: (0, 1), 0: (1, 0), 3: (1, 1)}[k]
                if fused:
                    weights = u_ref[0, place_of[0], place_of[1], group]
                else:
                    weights = u_ref[0, place_of[0], place_of[1]].reshape(depth, GATES)
                made[k] = dot(v_ref[k, m, ready : ready + depth], weights)
                for _ in range(share):
                    if waiting:
                        transform(*waiting.pop(0))
            for p in range(2):
                if group > 0:
                    other = pre_ref[0, p, m, :]
                elif first:
                    bias = jnp.concatenate([bias_ref[k : k + 1, :] for k in range(4)], axis=1)
                    other = dot(x_ref[p, m, :], w_ref[0]) + bias
                else:
                    other = before_ref[0, p, m, :]
                both = made[1] - made[2] if p else made[1] + made[2]
                edge = -made[3] if p else made[0]
                pre = 0.5 * both + edge + other
                if final and group == groups - 1:
                    gates(low, high, p, pre)
                else:
                    pre_ref[0, p, m, :] = pre


def run_pass(step, sizes, key, which, hidden, u, frame=None, before=None, cell=None, into=None):
    rows, cols, stride = sizes
    raw = isinstance(hidden, tuple)
    hiddens = hidden if raw else (hidden,)
    channels = hiddens[0].shape[2]
    first, final, fused = frame is not None, cell is not None, step == 0
    count = u.shape[4] // LANES if fused else u.shape[0]
    pairs = rows // 2 + (1 - step)
    height = up_to(pairs * stride, 16)
    middle = up_to(height // 2, 2 * stride if step else 16)
    tiles = ((0, middle), (middle, height))
    wide = up_to(max((rows // 2 + 2) * stride, height + stride + 2), 8)
    dims = (sizes, height, tiles, step, raw, first, final, int(into is not None))
    once = pl.Buffered(1)

    def whole(array):
        zeros = (0,) * array.ndim
        return pl.BlockSpec(array.shape, lambda n, k: zeros, pipeline_mode=once)

    def add(array, spec=None):
        args.append(array)
        in_specs.append(whole(array) if spec is None else spec)

    args, in_specs, aliases = [], [], {}
    for array in hiddens:
        block = array.shape[:2] + (channels,)
        add(array, pl.BlockSpec(block, lambda n, k: (0, 0, 0), pipeline_mode=once))
    if first:
        inner, *rims, w_in, biases = frame
        add(inner)
        for array in rims:
            block = array.shape[:2] + (LANES,)
            add(array, pl.BlockSpec(block, lambda n, k: (0, 0, count), pipeline_mode=once))
        add(w_in, pl.BlockSpec((1, w_in.shape[1], GATES), lambda n, k: (n, 0, 0)))
        add(biases, pl.BlockSpec((4, LANES), lambda n, k: (0, n)))
    else:
        add(before, pl.BlockSpec((1, 2, height, GATES), lambda n, k: (n, 0, 0, 0)))
    u_spec = pl.BlockSpec((1, 2, 2, 3, channels, GATES), lambda n, k: (n, 0, 0, 0, k[which], 0))
    if fused:
        add(u, pl.BlockSpec((3, 3, channels, 4, LANES), lambda n, k: (0, 0, k[which], 0, n)))
        if into is not None:
            aliases = {1 + len(args): 2 if final else 1}
            add(into, pl.BlockSpec(memory_space=pl.ANY))
    else:
        add(u, u_spec)
    if final and step == 0:
        for array, base in zip(cell, (0,) + (count + 1,) * 4):
            block = array.shape[:2] + (LANES,)
            add(array, pl.BlockSpec(block, lambda n, k, base=base: (0, 0, base + n)))
    elif final:
        add(cell, pl.BlockSpec((1,) + cell.shape[1:], lambda n, k: (n, 0, 0, 0)))
    scratch = [
        pltpu.VMEM((4, height, 3 * channels), BF16),
        pltpu.VMEM((2, wide, LANES), F32),
    ]
    if first:
        scratch.append(pltpu.VMEM((2, height, 6 * LANES), BF16))
    if final:
        scratch.append(pltpu.VMEM((1, 2, height, GATES), F32))
    if final and step == 0:
        scratch.append(pltpu.VMEM((1, 2, height, LANES), F32))
        scratch.append(pltpu.VMEM((2, height, LANES), F32))
    if fused:
        scratch.append(pltpu.VMEM((3, 4 * channels, LANES), F32))
    if not final:
        out_specs = [pl.BlockSpec((1, 2, height, GATES), lambda n, k: (n, 0, 0, 0))]
        out_shape = [jax.ShapeDtypeStruct((count, 2, height, GATES), F32)]
    elif step == 0:
        out_specs = [
            pl.BlockSpec((2, height, LANES), lambda n, k: (0, 0, n)),
            pl.BlockSpec((1, 2, height, LANES), lambda n, k: (n, 0, 0, 0)),
        ]
        out_shape = [
            jax.ShapeDtypeStruct((2, height, count * LANES), BF16),
            jax.ShapeDtypeStruct((count, 2, height, LANES), F32),
        ]
    else:
        shape = (rows, cols, count * LANES)
        out_specs = [pl.BlockSpec((rows, cols, LANES), lambda n, k: (0, 0, n))] * 2
        out_shape = [jax.ShapeDtypeStruct(shape, BF16), jax.ShapeDtypeStruct(shape, F32)]
    if fused:
        out_specs.append(u_spec)
        out_shape.append(jax.ShapeDtypeStruct((count, 2, 2, 3, 2 * channels, GATES), BF16))
    return pl.pallas_call(
        functools.partial(pass_kernel, dims),
        grid_spec=pltpu.PrefetchScalarGridSpec(
            num_scalar_prefetch=1,
            grid=(count,),
            in_specs=in_specs,
            out_specs=out_specs,
            scratch_shapes=scratch,
        ),
        out_shape=out_shape,
        input_output_aliases=aliases,
        compiler_params=params(),
        cost_estimate=pl.CostEstimate(
            flops=2 * height * count * GATES * 12 * channels,
            bytes_accessed=24 * channels * count * GATES,
            transcendentals=height * count * LANES * 10,
        ),
        name="step%d" % step,
    )(key, *args)


def forward(x, axis):
    count = lax.axis_size(axis)
    return lax.ppermute(x, axis, [(i, i + 1) for i in range(count - 1)])


def backward(x, axis):
    count = lax.axis_size(axis)
    return lax.ppermute(x, axis, [(i + 1, i) for i in range(count - 1)])


def swapped(x):
    return lax.ppermute(x, "ch", [(0, 1), (1, 0)])


def split(x):
    high = lax.reduce_precision(x, 8, 7)
    return high.astype(BF16), (x - high).astype(BF16)


def row_pack(hidden, frames, cell, two, one):
    ends = jnp.stack(split(cell[one]))
    return jnp.concatenate([hidden[two : two + 2], frames[two : two + 2], ends], axis=2)


def col_pack(hidden, frames, cell, north, south, two, one):
    rows, _, width = hidden.shape
    main = width + frames.shape[2]
    ends = jnp.stack(split(cell[:, one]), axis=1)
    middle = jnp.concatenate([hidden[:, two : two + 2], frames[:, two : two + 2], ends], axis=2)
    none = jnp.zeros((1, 2, width), BF16)
    upper = jnp.concatenate([none, north[None, :, one, main:]], axis=0)
    lower = jnp.concatenate([south[None, :, one, main:], none], axis=0)
    upper = jnp.concatenate([north[:, two : two + 2, :main], upper], axis=2)
    lower = jnp.concatenate([south[:, two : two + 2, :main], lower], axis=2)
    strip = jnp.concatenate([upper, middle, lower], axis=0)
    strip = strip.reshape(rows // 2 + 2, 2, 2, -1).transpose(2, 1, 0, 3)
    return strip.reshape(4, rows // 2 + 2, -1)


def per_device(frames, w_input, w_hidden, biases, hidden_init, cell_init):
    rows, cols, width = hidden_init.shape
    stride = up_to(cols + 4, 8)
    sizes = (rows, cols, stride)
    count = lax.axis_size("ch")
    paired = count == 2
    gather = lambda x: lax.all_gather(x, "ch", axis=x.ndim - 1, tiled=True)
    other = swapped(hidden_init) if paired else gather(hidden_init)
    local = (hidden_init, frames, cell_init)
    to_south = row_pack(*local, rows - 2, rows - 1)
    to_north = row_pack(*local, 0, 0)
    north, south = forward(to_south, "sy"), backward(to_north, "sy")
    to_east = col_pack(*local, north, south, cols - 2, cols - 1)
    to_west = col_pack(*local, north, south, 0, 0)
    west, east = forward(to_east, "sx"), backward(to_west, "sx")
    w_in = input_weights(w_input, to_east, to_west)
    rims = (north, south, west, east)
    frame = (frames, *rims, w_in, biases)
    cell = (cell_init, *rims)
    if paired:
        me = lax.axis_index("ch").astype(jnp.int32)
        halves = (me, 1 - me)
        hiddens = ((hidden_init, *rims), (other, *[swapped(rim) for rim in rims]))
    else:
        halves = (jnp.int32(0), jnp.int32(1))
        full = [other] + [gather(rim[:, :, :width]) for rim in rims]
        cut = other.shape[2] // 2
        hiddens = [tuple(x[:, :, k * cut : k * cut + cut] for x in full) for k in range(2)]
    y, x = lax.axis_index("sy"), lax.axis_index("sx")
    beside = [y > 0, y < lax.axis_size("sy") - 1, x > 0, x < lax.axis_size("sx") - 1]
    key = jnp.stack(list(halves) + [b.astype(jnp.int32) for b in beside])
    w = w_hidden.reshape((3, 3) + w_hidden.shape[1:])
    before, u = run_pass(0, sizes, key, 0, hiddens[0], w, frame=frame)
    hidden, cell, u = run_pass(
        0, sizes, key, 1, hiddens[1], w, before=before, cell=cell, into=u
    )
    if paired:
        hiddens = (hidden, swapped(hidden))
    else:
        full = gather(hidden)
        hiddens = [full[:, :, k * cut : k * cut + cut] for k in range(2)]
    (before,) = run_pass(1, sizes, key, 0, hiddens[0], u, frame=frame)
    return tuple(run_pass(1, sizes, key, 1, hiddens[1], u, before=before, cell=cell))


def solution(mesh):
    in_specs = (
        P("sy", "sx", None),
        P(None, None, None, "ch"),
        P(None, None, None, "ch"),
        P(None, "ch"),
        P("sy", "sx", "ch"),
        P("sy", "sx", "ch"),
    )
    out_specs = (P("sy", "sx", "ch"), P("sy", "sx", "ch"))
    return jax.shard_map(
        per_device, mesh=mesh, in_specs=in_specs, out_specs=out_specs, check_vma=False
    )
```

```python
import functools

import jax
import jax.numpy as jnp
from jax import lax
from jax.experimental import pallas as pl
from jax.experimental.pallas import tpu as pltpu
from jax.sharding import PartitionSpec as P

STEPS = 2
LANES = 128
GATES = 4 * LANES
F32 = jnp.float32
BF16 = jnp.bfloat16
VMEM = 60 * 2**20


def up_to(value, multiple):
    return -(-value // multiple) * multiple


def params():
    return pltpu.CompilerParams(vmem_limit_bytes=VMEM)


def input_weights_kernel(depth, blocks, w_ref, *refs):
    out_ref, wide_ref = refs[-2:]
    for j in range(blocks):
        lanes = slice(LANES * j, LANES * j + LANES)
        for b in range(3):
            wide_ref[b] = w_ref[0, b, :, :, lanes].astype(F32).reshape(depth * 4, LANES)
        for gate in range(4):
            out = slice(LANES * gate, LANES * gate + LANES)
            for b in range(3):
                rows = wide_ref[b, pl.ds(gate, depth, stride=4), :]
                out_ref[j, depth * b : depth * b + depth, out] = rows.astype(BF16)
        out_ref[j, 3 * depth :, :] = jnp.zeros((depth, GATES), BF16)


def input_weights(w_input, *after):
    _, depth, _, width = w_input.shape
    blocks = width // LANES
    return pl.pallas_call(
        functools.partial(input_weights_kernel, depth, blocks),
        grid=(3,),
        in_specs=[pl.BlockSpec((1, 3, depth, 4, width), lambda a: (a, 0, 0, 0, 0))]
        + [pl.BlockSpec(memory_space=pl.ANY)] * len(after),
        out_specs=pl.BlockSpec((blocks, 4 * depth, GATES), lambda a: (0, a, 0)),
        out_shape=jax.ShapeDtypeStruct((blocks, 12 * depth, GATES), BF16),
        scratch_shapes=[pltpu.VMEM((3, depth * 4, LANES), F32)],
        compiler_params=params(),
        cost_estimate=pl.CostEstimate(
            flops=0, bytes_accessed=48 * depth * 4 * width, transcendentals=0
        ),
        name="input_weights",
    )(w_input.reshape(3, 3, depth, 4, width), *after)


def sigmoid(x):
    return 0.5 * jnp.tanh(0.5 * x) + 0.5


def place(out_ref, origin, sizes, inner, rim_row, rim_col):
    rows, cols, stride = sizes
    for y in range(-origin, rows + origin):
        at = y + origin
        start = stride * (at // 2) + origin
        if y < 0:
            row = rim_row(0, y + 2)
        elif y >= rows:
            row = rim_row(1, y - rows)
        else:
            row = inner(y)
        out_ref[at % 2, start : start + cols, :] = row
    pairs = rows // 2 + origin
    for p in range(2):
        skip = (p + 2 - origin) // 2
        for k in range(origin):
            left = rim_col(0, 2 - origin + k, (p - origin) % 2)
            right = rim_col(1, k, (p - origin) % 2)
            out_ref[p, pl.ds(k, pairs, stride=stride), :] = left[skip : skip + pairs]
            at = origin + cols + k
            out_ref[p, pl.ds(at, pairs, stride=stride), :] = right[skip : skip + pairs]


def pass_kernel(dims, *refs):
    sizes, height, tiles, step, raw, first, final, into, which = dims
    rows, cols, stride = sizes
    fused = step == 0
    key_ref, refs = refs[0], list(refs[1:])
    take = lambda count: [refs.pop(0) for _ in range(count)]
    hidden_refs = take(5 if raw else 1)
    if first:
        frame_refs = take(5)
        w_ref, bias_ref = take(2)
    else:
        (before_ref,) = take(1)
    (u_ref,) = take(1)
    if fused:
        raw_ref = u_ref
        take(into)
    if final and step == 0:
        cell_refs = take(5)
    elif final:
        (cell_ref,) = take(1)
    if final:
        hidden_out, cell_out = take(2)
    else:
        (pre_ref,) = take(1)
    if fused:
        (made_ref,) = take(1)
    v_ref, wide_ref = take(2)
    if first:
        (x_ref,) = take(1)
    if final and step == 0:
        cell_ref, mask_ref = take(2)
    if fused:
        flat_ref, u_ref, copied = take(3)
    channels = v_ref.shape[2] // 3

    def surrounded(tile_refs, lanes):
        inner_ref, rows_refs, cols_refs = tile_refs[0], tile_refs[1:3], tile_refs[3:5]
        return (
            lambda y: inner_ref[y, :, lanes].astype(F32),
            lambda side, k: rows_refs[side][k, :, lanes].astype(F32),
            lambda side, k, p: cols_refs[side][2 * k + p, :, lanes].astype(F32),
        )

    def build_x():
        place(wide_ref, 2 - step, sizes, *surrounded(frame_refs, slice(None)))
        chunk = 48 if height % 48 == 0 else 16
        low = lax.broadcasted_iota(jnp.int32, (chunk, LANES), 1) < LANES // 2
        for q in range(2):
            for pair in range(2):
                for r in range(0, height, chunk):
                    start = stride * pair + r
                    at = [wide_ref[q, start + b : start + b + chunk, :] for b in range(3)]
                    turned = [pltpu.roll(value, LANES // 2, 1) for value in at]
                    if step == 0:
                        two, one = jnp.where(low, at[0], turned[1]), at[2]
                    else:
                        two, one = jnp.where(low, turned[0], at[1]), turned[2]
                    two, one = two.astype(BF16), one.astype(BF16)
                    rows = slice(r, r + chunk)
                    for p in range(2):
                        a = 2 * pair + q - p
                        if 0 <= a < 3:
                            x_ref[p, rows, 256 * a : 256 * a + LANES] = two
                            x_ref[p, rows, 256 * a + LANES : 256 * a + 256] = one

    def build_v(b, to):
        chunk = 48 if height % 48 == 0 else 16
        to = pl.ds(to, LANES)
        for r in range(0, height, chunk):
            near, far = slice(b + r, b + r + chunk), slice(stride + b + r, stride + b + r + chunk)
            d0, d1 = wide_ref[0, near, :], wide_ref[1, near, :]
            d2, d3 = wide_ref[0, far, :], wide_ref[1, far, :]
            rows = slice(r, r + chunk)
            v_ref[0, rows, to] = (d0 - d2).astype(BF16)
            v_ref[1, rows, to] = (d1 + d2).astype(BF16)
            v_ref[2, rows, to] = (d2 - d1).astype(BF16)
            v_ref[3, rows, to] = (d1 - d3).astype(BF16)

    def transform(b, c, chunk):
        rows = slice(c, c + chunk)
        for a in range(3):
            taken = raw_ref[a, b, rows, :, :].astype(F32)
            flat_ref[a, 4 * c : 4 * (c + chunk), :] = taken.reshape(4 * chunk, LANES)
        for gate in range(4):
            at = pl.ds(4 * c + gate, chunk, stride=4)
            g0, g1, g2 = [flat_ref[a, at, :] for a in range(3)]
            ends = g0 + g2
            out = slice(LANES * gate, LANES * gate + LANES)
            u_ref[0, 0, 0, b, rows, out] = (ends + g1).astype(BF16)
            u_ref[0, 0, 1, b, rows, out] = (ends - g1).astype(BF16)
            u_ref[0, 1, 0, b, rows, out] = g0.astype(BF16)
            u_ref[0, 1, 1, b, rows, out] = g2.astype(BF16)

    @pl.when(pl.program_id(0) == 0)
    def _():
        wide_ref[...] = jnp.zeros(wide_ref.shape, F32)
        if first:
            build_x()

        @pl.loop(0, channels // LANES)
        def _(j):
            lanes = pl.ds(pl.multiple_of(j * LANES, LANES), LANES)
            if raw:
                place(wide_ref, 2, sizes, *surrounded(hidden_refs, lanes))
            else:
                (hidden_ref,) = hidden_refs
                wide_ref[:, : hidden_ref.shape[1], :] = hidden_ref[:, :, lanes].astype(F32)
            for b in range(3):
                build_v(b, pl.multiple_of(b * channels + j * LANES, LANES))

        if final and step == 0:
            mask_ref[...] = jnp.zeros(mask_ref.shape, F32)
            edge = lambda k, length: jnp.where(key_ref[2 + k] > 0, jnp.ones((length, LANES), F32), 0)
            place(
                mask_ref,
                1,
                sizes,
                lambda y: jnp.ones((cols, LANES), F32),
                lambda side, k: edge(side, cols),
                lambda side, k, p: edge(2 + side, rows // 2 + 2),
            )
            low, high = slice(0, stride), slice(rows // 2 * stride, rows // 2 * stride + stride)
            mask_ref[0, low, :] = jnp.where(key_ref[2] > 0, mask_ref[0, low, :], 0)
            mask_ref[1, high, :] = jnp.where(key_ref[3] > 0, mask_ref[1, high, :], 0)

    if final and step == 0:
        cell_ref[0] = jnp.zeros(cell_ref.shape[1:], F32)
        inner, rim_row, rim_col = surrounded(cell_refs, slice(None))
        place(
            cell_ref.at[0],
            1,
            sizes,
            inner,
            lambda side, k: rim_row(side, 0) + rim_row(side, 1),
            lambda side, k, p: rim_col(side, 0, p) + rim_col(side, 1, p),
        )

    def dot(a, b):
        return jnp.dot(a, b, preferred_element_type=F32)

    def gates(low, high, p, pre):
        m = slice(low, high)
        i, f, o, g = [pre[:, LANES * k : LANES * k + LANES] for k in range(4)]
        if step == 0:
            before = cell_ref[0, p, m, :]
        else:
            skip = 1 + stride * p
            before = cell_ref[0, 1 - p, low + skip : high + skip, :]
        cell = sigmoid(f) * before + sigmoid(i) * jnp.tanh(g)
        hidden = sigmoid(o) * jnp.tanh(cell)
        if step == 0:
            cell_out[0, p, m, :] = cell
            hidden_out[p, m, :] = jnp.where(mask_ref[p, m, :] > 0, hidden, 0).astype(BF16)
        else:
            for t in range(low // stride, high // stride):
                r = slice(t * stride - low, t * stride - low + cols)
                cell_out[2 * t + p] = cell[r]
                hidden_out[2 * t + p] = hidden[r].astype(BF16)

    n = pl.program_id(0)

    def leave(block, b):
        half = pl.ds(pl.multiple_of(key_ref[which] * channels, channels), channels)
        return pltpu.make_async_copy(
            u_ref.at[0, :, :, b], made_ref.at[block, :, :, b, half, :], copied.at[b]
        )

    if fused:
        chunk = 32
        for b in range(3):

            @pl.when(n > 0)
            def _(b=b):
                leave(n - 1, b).wait()

            for c in range(0, channels, chunk):
                transform(b, c, chunk)
            leave(n, b).start()
    depth = 3 * channels
    for low, high in tiles:
        m = slice(low, high)
        made = {}
        for k, s, t in ((1, 0, 0), (2, 0, 1), (0, 1, 0), (3, 1, 1)):
            made[k] = dot(v_ref[k, m, :], u_ref[0, s, t].reshape(depth, GATES))
        for p in range(2):
            if first:
                bias = jnp.concatenate([bias_ref[k : k + 1, :] for k in range(4)], axis=1)
                other = dot(x_ref[p, m, :], w_ref[0]) + bias
            else:
                other = before_ref[0, p, m, :]
            both = made[1] - made[2] if p else made[1] + made[2]
            edge = -made[3] if p else made[0]
            pre = 0.5 * both + edge + other
            if final:
                gates(low, high, p, pre)
            else:
                pre_ref[0, p, m, :] = pre
    if fused:

        @pl.when(n == pl.num_programs(0) - 1)
        def _():
            for b in range(3):
                leave(n, b).wait()


def run_pass(step, sizes, key, which, hidden, u, frame=None, before=None, cell=None, into=None):
    rows, cols, stride = sizes
    raw = isinstance(hidden, tuple)
    hiddens = hidden if raw else (hidden,)
    channels = hiddens[0].shape[2]
    first, final, fused = frame is not None, cell is not None, step == 0
    count = u.shape[4] // LANES if fused else u.shape[0]
    pairs = rows // 2 + (1 - step)
    height = up_to(pairs * stride, 16)
    middle = up_to(height // 2, 2 * stride if step else 16)
    tiles = ((0, middle), (middle, height))
    wide = up_to(max((rows // 2 + 2) * stride, height + stride + 2), 8)
    dims = (sizes, height, tiles, step, raw, first, final, int(into is not None), which)
    once = pl.Buffered(1)

    def whole(array):
        zeros = (0,) * array.ndim
        return pl.BlockSpec(array.shape, lambda n, k: zeros, pipeline_mode=once)

    def add(array, spec=None):
        args.append(array)
        in_specs.append(whole(array) if spec is None else spec)

    args, in_specs, aliases = [], [], {}
    for array in hiddens:
        block = array.shape[:2] + (channels,)
        add(array, pl.BlockSpec(block, lambda n, k: (0, 0, 0), pipeline_mode=once))
    if first:
        inner, *rims, w_in, biases = frame
        add(inner)
        for array in rims:
            block = array.shape[:2] + (LANES,)
            add(array, pl.BlockSpec(block, lambda n, k: (0, 0, count), pipeline_mode=once))
        add(w_in, pl.BlockSpec((1, w_in.shape[1], GATES), lambda n, k: (n, 0, 0)))
        add(biases, pl.BlockSpec((4, LANES), lambda n, k: (0, n)))
    else:
        add(before, pl.BlockSpec((1, 2, height, GATES), lambda n, k: (n, 0, 0, 0)))
    u_spec = pl.BlockSpec((1, 2, 2, 3, channels, GATES), lambda n, k: (n, 0, 0, 0, k[which], 0))
    if fused:
        add(u, pl.BlockSpec((3, 3, channels, 4, LANES), lambda n, k: (0, 0, k[which], 0, n)))
        if into is not None:
            aliases = {1 + len(args): 2 if final else 1}
            add(into, pl.BlockSpec(memory_space=pl.ANY))
    else:
        add(u, u_spec)
    if final and step == 0:
        for array, base in zip(cell, (0,) + (count + 1,) * 4):
            block = array.shape[:2] + (LANES,)
            add(array, pl.BlockSpec(block, lambda n, k, base=base: (0, 0, base + n)))
    elif final:
        add(cell, pl.BlockSpec((1,) + cell.shape[1:], lambda n, k: (n, 0, 0, 0)))
    scratch = [
        pltpu.VMEM((4, height, 3 * channels), BF16),
        pltpu.VMEM((2, wide, LANES), F32),
    ]
    if first:
        scratch.append(pltpu.VMEM((2, height, 6 * LANES), BF16))
    if final and step == 0:
        scratch.append(pltpu.VMEM((1, 2, height, LANES), F32))
        scratch.append(pltpu.VMEM((2, height, LANES), F32))
    if fused:
        scratch.append(pltpu.VMEM((3, 4 * channels, LANES), F32))
        scratch.append(pltpu.VMEM((1, 2, 2, 3, channels, GATES), BF16))
        scratch.append(pltpu.SemaphoreType.DMA((3,)))
    if not final:
        out_specs = [pl.BlockSpec((1, 2, height, GATES), lambda n, k: (n, 0, 0, 0))]
        out_shape = [jax.ShapeDtypeStruct((count, 2, height, GATES), F32)]
    elif step == 0:
        out_specs = [
            pl.BlockSpec((2, height, LANES), lambda n, k: (0, 0, n)),
            pl.BlockSpec((1, 2, height, LANES), lambda n, k: (n, 0, 0, 0)),
        ]
        out_shape = [
            jax.ShapeDtypeStruct((2, height, count * LANES), BF16),
            jax.ShapeDtypeStruct((count, 2, height, LANES), F32),
        ]
    else:
        shape = (rows, cols, count * LANES)
        out_specs = [pl.BlockSpec((rows, cols, LANES), lambda n, k: (0, 0, n))] * 2
        out_shape = [jax.ShapeDtypeStruct(shape, BF16), jax.ShapeDtypeStruct(shape, F32)]
    if fused:
        out_specs.append(pl.BlockSpec(memory_space=pl.ANY))
        out_shape.append(jax.ShapeDtypeStruct((count, 2, 2, 3, 2 * channels, GATES), BF16))
    return pl.pallas_call(
        functools.partial(pass_kernel, dims),
        grid_spec=pltpu.PrefetchScalarGridSpec(
            num_scalar_prefetch=1,
            grid=(count,),
            in_specs=in_specs,
            out_specs=out_specs,
            scratch_shapes=scratch,
        ),
        out_shape=out_shape,
        input_output_aliases=aliases,
        compiler_params=params(),
        cost_estimate=pl.CostEstimate(
            flops=2 * height * count * GATES * 12 * channels,
            bytes_accessed=24 * channels * count * GATES,
            transcendentals=height * count * LANES * 10,
        ),
        name="step%d" % step,
    )(key, *args)


def forward(x, axis):
    count = lax.axis_size(axis)
    return lax.ppermute(x, axis, [(i, i + 1) for i in range(count - 1)])


def backward(x, axis):
    count = lax.axis_size(axis)
    return lax.ppermute(x, axis, [(i + 1, i) for i in range(count - 1)])


def swapped(x):
    return lax.ppermute(x, "ch", [(0, 1), (1, 0)])


def split(x):
    high = lax.reduce_precision(x, 8, 7)
    return high.astype(BF16), (x - high).astype(BF16)


def row_pack(hidden, frames, cell, two, one):
    ends = jnp.stack(split(cell[one]))
    return jnp.concatenate([hidden[two : two + 2], frames[two : two + 2], ends], axis=2)


def col_pack(hidden, frames, cell, north, south, two, one):
    rows, _, width = hidden.shape
    main = width + frames.shape[2]
    ends = jnp.stack(split(cell[:, one]), axis=1)
    middle = jnp.concatenate([hidden[:, two : two + 2], frames[:, two : two + 2], ends], axis=2)
    none = jnp.zeros((1, 2, width), BF16)
    upper = jnp.concatenate([none, north[None, :, one, main:]], axis=0)
    lower = jnp.concatenate([south[None, :, one, main:], none], axis=0)
    upper = jnp.concatenate([north[:, two : two + 2, :main], upper], axis=2)
    lower = jnp.concatenate([south[:, two : two + 2, :main], lower], axis=2)
    strip = jnp.concatenate([upper, middle, lower], axis=0)
    strip = strip.reshape(rows // 2 + 2, 2, 2, -1).transpose(2, 1, 0, 3)
    return strip.reshape(4, rows // 2 + 2, -1)


def per_device(frames, w_input, w_hidden, biases, hidden_init, cell_init):
    rows, cols, width = hidden_init.shape
    stride = up_to(cols + 4, 8)
    sizes = (rows, cols, stride)
    count = lax.axis_size("ch")
    paired = count == 2
    gather = lambda x: lax.all_gather(x, "ch", axis=x.ndim - 1, tiled=True)
    other = swapped(hidden_init) if paired else gather(hidden_init)
    local = (hidden_init, frames, cell_init)
    to_south = row_pack(*local, rows - 2, rows - 1)
    to_north = row_pack(*local, 0, 0)
    north, south = forward(to_south, "sy"), backward(to_north, "sy")
    to_east = col_pack(*local, north, south, cols - 2, cols - 1)
    to_west = col_pack(*local, north, south, 0, 0)
    west, east = forward(to_east, "sx"), backward(to_west, "sx")
    w_in = input_weights(w_input, to_east, to_west)
    rims = (north, south, west, east)
    frame = (frames, *rims, w_in, biases)
    cell = (cell_init, *rims)
    if paired:
        me = lax.axis_index("ch").astype(jnp.int32)
        halves = (me, 1 - me)
        hiddens = ((hidden_init, *rims), (other, *[swapped(rim) for rim in rims]))
    else:
        halves = (jnp.int32(0), jnp.int32(1))
        full = [other] + [gather(rim[:, :, :width]) for rim in rims]
        cut = other.shape[2] // 2
        hiddens = [tuple(x[:, :, k * cut : k * cut + cut] for x in full) for k in range(2)]
    y, x = lax.axis_index("sy"), lax.axis_index("sx")
    beside = [y > 0, y < lax.axis_size("sy") - 1, x > 0, x < lax.axis_size("sx") - 1]
    key = jnp.stack(list(halves) + [b.astype(jnp.int32) for b in beside])
    w = w_hidden.reshape((3, 3) + w_hidden.shape[1:])
    before, u = run_pass(0, sizes, key, 0, hiddens[0], w, frame=frame)
    hidden, cell, u = run_pass(
        0, sizes, key, 1, hiddens[1], w, before=before, cell=cell, into=u
    )
    if paired:
        hiddens = (hidden, swapped(hidden))
    else:
        full = gather(hidden)
        hiddens = [full[:, :, k * cut : k * cut + cut] for k in range(2)]
    (before,) = run_pass(1, sizes, key, 0, hiddens[0], u, frame=frame)
    return tuple(run_pass(1, sizes, key, 1, hiddens[1], u, before=before, cell=cell))


def solution(mesh):
    in_specs = (
        P("sy", "sx", None),
        P(None, None, None, "ch"),
        P(None, None, None, "ch"),
        P(None, "ch"),
        P("sy", "sx", "ch"),
        P("sy", "sx", "ch"),
    )
    out_specs = (P("sy", "sx", "ch"), P("sy", "sx", "ch"))
    return jax.shard_map(
        per_device, mesh=mesh, in_specs=in_specs, out_specs=out_specs, check_vma=False
    )
```

```python
import functools

import jax
import jax.numpy as jnp
from jax import lax
from jax.experimental import pallas as pl
from jax.experimental.pallas import tpu as pltpu
from jax.sharding import PartitionSpec as P

STEPS = 2
LANES = 128
GATES = 4 * LANES
F32 = jnp.float32
BF16 = jnp.bfloat16
VMEM = 60 * 2**20


def up_to(value, multiple):
    return -(-value // multiple) * multiple


def params():
    return pltpu.CompilerParams(vmem_limit_bytes=VMEM)


def input_weights_kernel(depth, blocks, w_ref, *refs):
    out_ref, wide_ref = refs[-2:]
    for j in range(blocks):
        lanes = slice(LANES * j, LANES * j + LANES)
        for b in range(3):
            for c in range(0, depth, 32):
                taken = w_ref[0, b, c : c + 32, :, lanes].astype(F32)
                wide_ref[b, 4 * c : 4 * c + 128, :] = taken.reshape(128, LANES)
                for gate in range(4):
                    out = slice(LANES * gate, LANES * gate + LANES)
                    rows = wide_ref[b, pl.ds(4 * c + gate, 32, stride=4), :]
                    out_ref[j, depth * b + c : depth * b + c + 32, out] = rows.astype(BF16)
        out_ref[j, 3 * depth :, :] = jnp.zeros((depth, GATES), BF16)


def input_weights(w_input, *after):
    _, depth, _, width = w_input.shape
    blocks = width // LANES
    return pl.pallas_call(
        functools.partial(input_weights_kernel, depth, blocks),
        grid=(3,),
        in_specs=[pl.BlockSpec((1, 3, depth, 4, width), lambda a: (a, 0, 0, 0, 0))]
        + [pl.BlockSpec(memory_space=pl.ANY)] * len(after),
        out_specs=pl.BlockSpec((blocks, 4 * depth, GATES), lambda a: (0, a, 0)),
        out_shape=jax.ShapeDtypeStruct((blocks, 12 * depth, GATES), BF16),
        scratch_shapes=[pltpu.VMEM((3, depth * 4, LANES), F32)],
        compiler_params=params(),
        cost_estimate=pl.CostEstimate(
            flops=0, bytes_accessed=48 * depth * 4 * width, transcendentals=0
        ),
        name="input_weights",
    )(w_input.reshape(3, 3, depth, 4, width), *after)


def sigmoid(x):
    return 0.5 * jnp.tanh(0.5 * x) + 0.5


def place(out_ref, origin, sizes, inner, rim_row, rim_col):
    rows, cols, stride = sizes
    for y in range(-origin, rows + origin):
        at = y + origin
        start = stride * (at // 2) + origin
        if y < 0:
            row = rim_row(0, y + 2)
        elif y >= rows:
            row = rim_row(1, y - rows)
        else:
            row = inner(y)
        out_ref[at % 2, start : start + cols, :] = row
    pairs = rows // 2 + origin
    for p in range(2):
        skip = (p + 2 - origin) // 2
        for k in range(origin):
            left = rim_col(0, 2 - origin + k, (p - origin) % 2)
            right = rim_col(1, k, (p - origin) % 2)
            out_ref[p, pl.ds(k, pairs, stride=stride), :] = left[skip : skip + pairs]
            at = origin + cols + k
            out_ref[p, pl.ds(at, pairs, stride=stride), :] = right[skip : skip + pairs]


def pass_kernel(dims, *refs):
    sizes, height, tiles, step, raw, first, final, into, which = dims
    rows, cols, stride = sizes
    fused = step == 0
    key_ref, refs = refs[0], list(refs[1:])
    take = lambda count: [refs.pop(0) for _ in range(count)]
    hidden_refs = take(5 if raw else 1)
    if first:
        frame_refs = take(5)
        w_ref, bias_ref = take(2)
    else:
        (before_ref,) = take(1)
    (u_ref,) = take(1)
    if fused:
        raw_ref = u_ref
        take(into)
    if final and step == 0:
        cell_refs = take(5)
    elif final:
        (cell_ref,) = take(1)
    if final:
        hidden_out, cell_out = take(2)
    else:
        (pre_ref,) = take(1)
    if fused:
        (made_ref,) = take(1)
    v_ref, wide_ref = take(2)
    if first:
        (x_ref,) = take(1)
    if final and step == 0:
        cell_ref, mask_ref = take(2)
    if fused:
        flat_ref, u_ref, copied = take(3)
    channels = v_ref.shape[2] // 3

    def surrounded(tile_refs, lanes):
        inner_ref, rows_refs, cols_refs = tile_refs[0], tile_refs[1:3], tile_refs[3:5]
        return (
            lambda y: inner_ref[y, :, lanes].astype(F32),
            lambda side, k: rows_refs[side][k, :, lanes].astype(F32),
            lambda side, k, p: cols_refs[side][2 * k + p, :, lanes].astype(F32),
        )

    def build_x():
        place(wide_ref, 2 - step, sizes, *surrounded(frame_refs, slice(None)))
        chunk = 48 if height % 48 == 0 else 16
        low = lax.broadcasted_iota(jnp.int32, (chunk, LANES), 1) < LANES // 2
        for q in range(2):
            for pair in range(2):
                for r in range(0, height, chunk):
                    start = stride * pair + r
                    at = [wide_ref[q, start + b : start + b + chunk, :] for b in range(3)]
                    turned = [pltpu.roll(value, LANES // 2, 1) for value in at]
                    if step == 0:
                        two, one = jnp.where(low, at[0], turned[1]), at[2]
                    else:
                        two, one = jnp.where(low, turned[0], at[1]), turned[2]
                    two, one = two.astype(BF16), one.astype(BF16)
                    rows = slice(r, r + chunk)
                    for p in range(2):
                        a = 2 * pair + q - p
                        if 0 <= a < 3:
                            x_ref[p, rows, 256 * a : 256 * a + LANES] = two
                            x_ref[p, rows, 256 * a + LANES : 256 * a + 256] = one

    def build_v(b, to):
        chunk = 48 if height % 48 == 0 else 16
        to = pl.ds(to, LANES)
        for r in range(0, height, chunk):
            near, far = slice(b + r, b + r + chunk), slice(stride + b + r, stride + b + r + chunk)
            d0, d1 = wide_ref[0, near, :], wide_ref[1, near, :]
            d2, d3 = wide_ref[0, far, :], wide_ref[1, far, :]
            rows = slice(r, r + chunk)
            v_ref[0, rows, to] = (d0 - d2).astype(BF16)
            v_ref[1, rows, to] = (d1 + d2).astype(BF16)
            v_ref[2, rows, to] = (d2 - d1).astype(BF16)
            v_ref[3, rows, to] = (d1 - d3).astype(BF16)

    def transform(b, c, chunk):
        rows = slice(c, c + chunk)
        for a in range(3):
            taken = raw_ref[a, b, rows, :, :].astype(F32)
            flat_ref[a, 4 * c : 4 * (c + chunk), :] = taken.reshape(4 * chunk, LANES)
        for gate in range(4):
            at = pl.ds(4 * c + gate, chunk, stride=4)
            g0, g1, g2 = [flat_ref[a, at, :] for a in range(3)]
            ends = g0 + g2
            out = slice(LANES * gate, LANES * gate + LANES)
            u_ref[0, 0, 0, b, rows, out] = (ends + g1).astype(BF16)
            u_ref[0, 0, 1, b, rows, out] = (ends - g1).astype(BF16)
            u_ref[0, 1, 0, b, rows, out] = g0.astype(BF16)
            u_ref[0, 1, 1, b, rows, out] = g2.astype(BF16)

    @pl.when(pl.program_id(0) == 0)
    def _():
        wide_ref[...] = jnp.zeros(wide_ref.shape, F32)
        if first:
            build_x()

        @pl.loop(0, channels // LANES)
        def _(j):
            lanes = pl.ds(pl.multiple_of(j * LANES, LANES), LANES)
            if raw:
                place(wide_ref, 2, sizes, *surrounded(hidden_refs, lanes))
            else:
                (hidden_ref,) = hidden_refs
                wide_ref[:, : hidden_ref.shape[1], :] = hidden_ref[:, :, lanes].astype(F32)
            for b in range(3):
                build_v(b, pl.multiple_of(b * channels + j * LANES, LANES))

        if final and step == 0:
            mask_ref[...] = jnp.zeros(mask_ref.shape, F32)
            edge = lambda k, length: jnp.where(key_ref[2 + k] > 0, jnp.ones((length, LANES), F32), 0)
            place(
                mask_ref,
                1,
                sizes,
                lambda y: jnp.ones((cols, LANES), F32),
                lambda side, k: edge(side, cols),
                lambda side, k, p: edge(2 + side, rows // 2 + 2),
            )
            low, high = slice(0, stride), slice(rows // 2 * stride, rows // 2 * stride + stride)
            mask_ref[0, low, :] = jnp.where(key_ref[2] > 0, mask_ref[0, low, :], 0)
            mask_ref[1, high, :] = jnp.where(key_ref[3] > 0, mask_ref[1, high, :], 0)

    if final and step == 0:
        cell_ref[0] = jnp.zeros(cell_ref.shape[1:], F32)
        inner, rim_row, rim_col = surrounded(cell_refs, slice(None))
        place(
            cell_ref.at[0],
            1,
            sizes,
            inner,
            lambda side, k: rim_row(side, 0) + rim_row(side, 1),
            lambda side, k, p: rim_col(side, 0, p) + rim_col(side, 1, p),
        )

    def dot(a, b):
        return jnp.dot(a, b, preferred_element_type=F32)

    def gates(low, high, p, pre):
        m = slice(low, high)
        i, f, o, g = [pre[:, LANES * k : LANES * k + LANES] for k in range(4)]
        if step == 0:
            before = cell_ref[0, p, m, :]
        else:
            skip = 1 + stride * p
            before = cell_ref[0, 1 - p, low + skip : high + skip, :]
        cell = sigmoid(f) * before + sigmoid(i) * jnp.tanh(g)
        hidden = sigmoid(o) * jnp.tanh(cell)
        if step == 0:
            cell_out[0, p, m, :] = cell
            hidden_out[p, m, :] = jnp.where(mask_ref[p, m, :] > 0, hidden, 0).astype(BF16)
        else:
            for t in range(low // stride, high // stride):
                r = slice(t * stride - low, t * stride - low + cols)
                cell_out[2 * t + p] = cell[r]
                hidden_out[2 * t + p] = hidden[r].astype(BF16)

    n = pl.program_id(0)

    def leave(block, b):
        half = pl.ds(pl.multiple_of(key_ref[which] * channels, channels), channels)
        return pltpu.make_async_copy(
            u_ref.at[0, :, :, b], made_ref.at[block, :, :, b, half, :], copied.at[b]
        )

    if fused:
        chunk = 32
        for b in range(3):

            @pl.when(n > 0)
            def _(b=b):
                leave(n - 1, b).wait()

            for c in range(0, channels, chunk):
                transform(b, c, chunk)
            leave(n, b).start()
    depth = 3 * channels
    for low, high in tiles:
        m = slice(low, high)
        made = {}
        for k, s, t in ((1, 0, 0), (2, 0, 1), (0, 1, 0), (3, 1, 1)):
            made[k] = dot(v_ref[k, m, :], u_ref[0, s, t].reshape(depth, GATES))
        for p in range(2):
            if first:
                bias = jnp.concatenate([bias_ref[k : k + 1, :] for k in range(4)], axis=1)
                other = dot(x_ref[p, m, :], w_ref[0]) + bias
            else:
                other = before_ref[0, p, m, :]
            both = made[1] - made[2] if p else made[1] + made[2]
            edge = -made[3] if p else made[0]
            pre = 0.5 * both + edge + other
            if final:
                gates(low, high, p, pre)
            else:
                pre_ref[0, p, m, :] = pre
    if fused:

        @pl.when(n == pl.num_programs(0) - 1)
        def _():
            for b in range(3):
                leave(n, b).wait()


def run_pass(step, sizes, key, which, hidden, u, frame=None, before=None, cell=None, into=None):
    rows, cols, stride = sizes
    raw = isinstance(hidden, tuple)
    hiddens = hidden if raw else (hidden,)
    channels = hiddens[0].shape[2]
    first, final, fused = frame is not None, cell is not None, step == 0
    count = u.shape[4] // LANES if fused else u.shape[0]
    pairs = rows // 2 + (1 - step)
    height = up_to(pairs * stride, 16)
    middle = up_to(height // 2, 2 * stride if step else 16)
    tiles = ((0, middle), (middle, height))
    wide = up_to(max((rows // 2 + 2) * stride, height + stride + 2), 8)
    dims = (sizes, height, tiles, step, raw, first, final, int(into is not None), which)
    once = pl.Buffered(1)

    def whole(array):
        zeros = (0,) * array.ndim
        return pl.BlockSpec(array.shape, lambda n, k: zeros, pipeline_mode=once)

    def add(array, spec=None):
        args.append(array)
        in_specs.append(whole(array) if spec is None else spec)

    args, in_specs, aliases = [], [], {}
    for place_of, array in enumerate(hiddens):
        joined = place_of >= 3 and array.shape[0] == 8
        block = (4 if joined else array.shape[0], array.shape[1], channels)
        side = place_of - 3 if joined else 0
        add(array, pl.BlockSpec(block, lambda n, k, side=side: (side, 0, 0), pipeline_mode=once))
    if first:
        inner, *rims, w_in, biases = frame
        add(inner)
        for array in rims:
            block = array.shape[:2] + (LANES,)
            add(array, pl.BlockSpec(block, lambda n, k: (0, 0, count), pipeline_mode=once))
        add(w_in, pl.BlockSpec((1, w_in.shape[1], GATES), lambda n, k: (n, 0, 0)))
        add(biases, pl.BlockSpec((4, LANES), lambda n, k: (0, n)))
    else:
        add(before, pl.BlockSpec((1, 2, height, GATES), lambda n, k: (n, 0, 0, 0)))
    u_spec = pl.BlockSpec((1, 2, 2, 3, channels, GATES), lambda n, k: (n, 0, 0, 0, k[which], 0))
    if fused:
        add(u, pl.BlockSpec((3, 3, channels, 4, LANES), lambda n, k: (0, 0, k[which], 0, n)))
        if into is not None:
            aliases = {1 + len(args): 2 if final else 1}
            add(into, pl.BlockSpec(memory_space=pl.ANY))
    else:
        add(u, u_spec)
    if final and step == 0:
        for array, base in zip(cell, (0,) + (count + 1,) * 4):
            block = array.shape[:2] + (LANES,)
            add(array, pl.BlockSpec(block, lambda n, k, base=base: (0, 0, base + n)))
    elif final:
        add(cell, pl.BlockSpec((1,) + cell.shape[1:], lambda n, k: (n, 0, 0, 0)))
    scratch = [
        pltpu.VMEM((4, height, 3 * channels), BF16),
        pltpu.VMEM((2, wide, LANES), F32),
    ]
    if first:
        scratch.append(pltpu.VMEM((2, height, 6 * LANES), BF16))
    if final and step == 0:
        scratch.append(pltpu.VMEM((1, 2, height, LANES), F32))
        scratch.append(pltpu.VMEM((2, height, LANES), F32))
    if fused:
        scratch.append(pltpu.VMEM((3, 4 * channels, LANES), F32))
        scratch.append(pltpu.VMEM((1, 2, 2, 3, channels, GATES), BF16))
        scratch.append(pltpu.SemaphoreType.DMA((3,)))
    if not final:
        out_specs = [pl.BlockSpec((1, 2, height, GATES), lambda n, k: (n, 0, 0, 0))]
        out_shape = [jax.ShapeDtypeStruct((count, 2, height, GATES), F32)]
    elif step == 0:
        out_specs = [
            pl.BlockSpec((2, height, LANES), lambda n, k: (0, 0, n)),
            pl.BlockSpec((1, 2, height, LANES), lambda n, k: (n, 0, 0, 0)),
        ]
        out_shape = [
            jax.ShapeDtypeStruct((2, height, count * LANES), BF16),
            jax.ShapeDtypeStruct((count, 2, height, LANES), F32),
        ]
    else:
        shape = (rows, cols, count * LANES)
        out_specs = [pl.BlockSpec((rows, cols, LANES), lambda n, k: (0, 0, n))] * 2
        out_shape = [jax.ShapeDtypeStruct(shape, BF16), jax.ShapeDtypeStruct(shape, F32)]
    if fused:
        out_specs.append(pl.BlockSpec(memory_space=pl.ANY))
        out_shape.append(jax.ShapeDtypeStruct((count, 2, 2, 3, 2 * channels, GATES), BF16))
    return pl.pallas_call(
        functools.partial(pass_kernel, dims),
        grid_spec=pltpu.PrefetchScalarGridSpec(
            num_scalar_prefetch=1,
            grid=(count,),
            in_specs=in_specs,
            out_specs=out_specs,
            scratch_shapes=scratch,
        ),
        out_shape=out_shape,
        input_output_aliases=aliases,
        compiler_params=params(),
        cost_estimate=pl.CostEstimate(
            flops=2 * height * count * GATES * 12 * channels,
            bytes_accessed=24 * channels * count * GATES,
            transcendentals=height * count * LANES * 10,
        ),
        name="step%d" % step,
    )(key, *args)


def forward(x, axis):
    count = lax.axis_size(axis)
    return lax.ppermute(x, axis, [(i, i + 1) for i in range(count - 1)])


def backward(x, axis):
    count = lax.axis_size(axis)
    return lax.ppermute(x, axis, [(i + 1, i) for i in range(count - 1)])


def swapped(x):
    return lax.ppermute(x, "ch", [(0, 1), (1, 0)])


def split(x):
    high = lax.reduce_precision(x, 8, 7)
    return high.astype(BF16), (x - high).astype(BF16)


def row_pack(hidden, frames, cell, two, one):
    ends = jnp.stack(split(cell[one]))
    return jnp.concatenate([hidden[two : two + 2], frames[two : two + 2], ends], axis=2)


def col_pack(hidden, frames, cell, north, south, two, one):
    rows, _, width = hidden.shape
    main = width + frames.shape[2]
    ends = jnp.stack(split(cell[:, one]), axis=1)
    middle = jnp.concatenate([hidden[:, two : two + 2], frames[:, two : two + 2], ends], axis=2)
    none = jnp.zeros((1, 2, width), BF16)
    upper = jnp.concatenate([none, north[None, :, one, main:]], axis=0)
    lower = jnp.concatenate([south[None, :, one, main:], none], axis=0)
    upper = jnp.concatenate([north[:, two : two + 2, :main], upper], axis=2)
    lower = jnp.concatenate([south[:, two : two + 2, :main], lower], axis=2)
    strip = jnp.concatenate([upper, middle, lower], axis=0)
    strip = strip.reshape(rows // 2 + 2, 2, 2, -1).transpose(2, 1, 0, 3)
    return strip.reshape(4, rows // 2 + 2, -1)


def per_device(frames, w_input, w_hidden, biases, hidden_init, cell_init):
    rows, cols, width = hidden_init.shape
    stride = up_to(cols + 4, 8)
    sizes = (rows, cols, stride)
    count = lax.axis_size("ch")
    paired = count == 2
    gather = lambda x: lax.all_gather(x, "ch", axis=x.ndim - 1, tiled=True)
    other = swapped(hidden_init) if paired else gather(hidden_init)
    local = (hidden_init, frames, cell_init)
    to_south = row_pack(*local, rows - 2, rows - 1)
    to_north = row_pack(*local, 0, 0)
    north, south = forward(to_south, "sy"), backward(to_north, "sy")
    to_east = col_pack(*local, north, south, cols - 2, cols - 1)
    to_west = col_pack(*local, north, south, 0, 0)
    west, east = forward(to_east, "sx"), backward(to_west, "sx")
    w_in = input_weights(w_input, to_east, to_west)
    rims = (north, south, west, east)
    frame = (frames, *rims, w_in, biases)
    cell = (cell_init, *rims)
    if paired:
        me = lax.axis_index("ch").astype(jnp.int32)
        halves = (me, 1 - me)
        sides = swapped(jnp.concatenate([west, east]))
        hiddens = (
            (hidden_init, *rims),
            (other, swapped(north), swapped(south), sides, sides),
        )
    else:
        halves = (jnp.int32(0), jnp.int32(1))
        full = [other] + [gather(rim[:, :, :width]) for rim in rims]
        cut = other.shape[2] // 2
        hiddens = [tuple(x[:, :, k * cut : k * cut + cut] for x in full) for k in range(2)]
    y, x = lax.axis_index("sy"), lax.axis_index("sx")
    beside = [y > 0, y < lax.axis_size("sy") - 1, x > 0, x < lax.axis_size("sx") - 1]
    key = jnp.stack(list(halves) + [b.astype(jnp.int32) for b in beside])
    w = w_hidden.reshape((3, 3) + w_hidden.shape[1:])
    before, u = run_pass(0, sizes, key, 0, hiddens[0], w, frame=frame)
    hidden, cell, u = run_pass(
        0, sizes, key, 1, hiddens[1], w, before=before, cell=cell, into=u
    )
    if paired:
        hiddens = (hidden, swapped(hidden))
    else:
        full = gather(hidden)
        hiddens = [full[:, :, k * cut : k * cut + cut] for k in range(2)]
    (before,) = run_pass(1, sizes, key, 0, hiddens[0], u, frame=frame)
    return tuple(run_pass(1, sizes, key, 1, hiddens[1], u, before=before, cell=cell))


def solution(mesh):
    in_specs = (
        P("sy", "sx", None),
        P(None, None, None, "ch"),
        P(None, None, None, "ch"),
        P(None, "ch"),
        P("sy", "sx", "ch"),
        P("sy", "sx", "ch"),
    )
    out_specs = (P("sy", "sx", "ch"), P("sy", "sx", "ch"))
    return jax.shard_map(
        per_device, mesh=mesh, in_specs=in_specs, out_specs=out_specs, check_vma=False
    )
```
